512 devices in a mesh: dp: 4 (over z_lo), slot: 128 (over x, z_hi, y, core).
Axes of the slice: x: 4, y: 8, z: 8 (z_hi: 2, z_lo: 4; z = z_hi * 4 + z_lo), core: 2. Of those that a mesh axis runs over, the one named last changes fastest.
Arguments:
- queries: bfloat16 [1024, 4096], P(('dp', 'slot')), may hold values from -25.5 to 25.5
- keys: bfloat16 [20480, 4096], P('slot'), may hold values from -7 to 7
- values: bfloat16 [20480, 4096], P('slot'), may hold values from -6 to 6
- cotangent: bfloat16 [1024, 4096], P(('dp', 'slot')), may hold values from -96 to 96
Outputs:
- query_grad: bfloat16 [1024, 4096], P(('dp', 'slot'))
- key_grad: bfloat16 [20480, 4096], P('slot')
- value_grad: bfloat16 [20480, 4096], P('slot')
The draws below stay inside these ranges and needn't reach their ends.
All inputs are finite; a program needn't handle non-finite values.
Results may differ from the reference program's by a relative error of at most 0.015.
Values may be sent and summed in bfloat16 or wider, within the bound.
A program may use at most 64 MiB of HBM per device.

```python
import jax
import jax.numpy as jnp

D = 4096
SLOTS = 20480
TOK_GROUP = 256
TOKENS = 1024
N_DP = 4


def key_rows(key):
    normal_part = jnp.clip(jax.random.normal(jax.random.fold_in(key, 11), (SLOTS, D), jnp.float32), -6.0, 6.0)
    base = normal_part
    leaders = base[0:32:2]
    followers = jnp.clip(leaders + base[1:32:2], -7.0, 7.0)
    paired = jnp.stack([leaders, followers], axis=1).reshape(32, D)
    return jnp.concatenate([paired, base[32:]], axis=0)


def draw_keys(key, part):
    return key_rows(key).astype(jnp.bfloat16)


def draw_queries(key, part):
    own_key = jax.random.fold_in(key, 5)
    drawn = jnp.clip(jax.random.normal(own_key, (TOKENS, D), jnp.float32), -6.0, 6.0)
    return drawn.astype(jnp.bfloat16)


def levels(stream_key, extent, shards, least, largest):
    gain = 1.0
    for position, blocks in shards:
        steps = jax.random.uniform(jax.random.fold_in(jax.random.fold_in(stream_key, 6), position), (blocks,), jnp.float32, least / len(shards), largest / len(shards))
        gain = gain * jnp.repeat(jnp.exp(steps), extent[position] // blocks).reshape((-1,) + (1,) * (len(extent) - 1 - position))
    return gain


def bell_draw(stream_key, extent, deviation, limit, split=(), kind=jnp.bfloat16):
    drawn = jax.random.normal(stream_key, extent, jnp.float32) * deviation
    if len(split) > 0:
        drawn = levels(stream_key, extent, split, -0.22, 0.18) * drawn
    return jnp.clip(drawn, min=-limit, max=limit).astype(kind)


def setup_inputs(seed: int = 0) -> dict:
    splits = jax.random.split(jax.random.key(seed), 5)
    return {
        "queries": draw_queries(jax.random.fold_in(splits[4], 71), 0),
        "keys": draw_keys(jax.random.fold_in(splits[4], 71), 0),
        "values": bell_draw(splits[2], (SLOTS, D), 1.0, 6.0, ((0, 128),)),
        "cotangent": bell_draw(splits[3], (TOKENS, D), 16.0, 96.0, ((0, 512),)),
    }


def reference(queries, keys, values, cotangent):
    beta = 1.25 * D ** -0.5
    keys_wide = keys.astype(jnp.float32)
    key_norm = jnp.sum(keys_wide * keys_wide, axis=1)
    query_parts = []
    key_total = jnp.zeros((SLOTS, D), jnp.float32)
    value_total = jnp.zeros((SLOTS, D), jnp.float32)
    for group in range(N_DP):
        rows_q = queries[group * TOK_GROUP:(group + 1) * TOK_GROUP]
        rows_g = cotangent[group * TOK_GROUP:(group + 1) * TOK_GROUP]
        scores = beta * jnp.dot(rows_q, keys.T, preferred_element_type=jnp.float32) - 0.5 * beta * key_norm[None, :]
        top = jnp.max(scores, axis=1, keepdims=True)
        lse = top + jnp.log(jnp.sum(jnp.exp(scores - top), axis=1, keepdims=True))
        prob = jnp.exp(scores - lse)
        dprob = jnp.dot(rows_g, values.T, preferred_element_type=jnp.float32)
        delta = jnp.sum(prob * dprob, axis=1, keepdims=True)
        dscore = (beta * prob * (dprob - delta)).astype(jnp.bfloat16)
        query_parts.append(jnp.dot(dscore, keys, preferred_element_type=jnp.float32).astype(jnp.bfloat16))
        value_part = jnp.dot(prob.astype(jnp.bfloat16).T, rows_g, preferred_element_type=jnp.float32).astype(jnp.bfloat16)
        column_sum = jnp.sum(dscore.astype(jnp.float32), axis=0)
        key_part = (jnp.dot(dscore.T, rows_q, preferred_element_type=jnp.float32) - column_sum[:, None] * keys_wide).astype(jnp.bfloat16)
        key_total = key_total + key_part.astype(jnp.float32)
        value_total = value_total + value_part.astype(jnp.float32)
    return jnp.concatenate(query_parts, axis=0), key_total.astype(jnp.bfloat16), value_total.astype(jnp.bfloat16)
```

```python
import jax
import jax.numpy as jnp
from jax import lax
from jax.experimental import pallas as pl
from jax.experimental.pallas import tpu as pltpu
from jax.sharding import PartitionSpec as P

MESH = pl.DeviceIdType.MESH
D = 4096
BETA = 1.25 * D ** (-0.5)
NX, NY, NZ, NDP = 4, 8, 8, 4
SL = 160
F = 512
NF = D // F
BF = jnp.bfloat16
F32 = jnp.float32

PLANE = (0, 4, 3, -3, 2, -2)

HOP_US = 1.9
CORE_HOP_US = 1.5
LINK_RATE = 48e3
CORE_RATE = 500e3


class Plan:
    def __init__(self):
        self.items = {}

    def transfer(self, name, needs, link, size, hops=1, rank=0):
        self.items[name] = dict(kind="t", needs=list(needs), link=link, size=size, hops=hops, rank=rank)

    def compute(self, name, needs, cost, rank=0):
        self.items[name] = dict(kind="c", needs=list(needs), cost=cost, rank=rank)

    def order(self):
        now = 0.0
        done, started, arrivals, free, steps = set(), set(), {}, {}, []
        while len(done) < len(self.items):
            ready = [
                n for n, i in self.items.items()
                if n not in started and all(d in done for d in i["needs"])
            ]
            sends = sorted((n for n in ready if self.items[n]["kind"] == "t"), key=lambda n: self.items[n]["rank"])
            for n in sends:
                i = self.items[n]
                rate, hop = (CORE_RATE, CORE_HOP_US) if i["link"] == "core" else (LINK_RATE, HOP_US)
                now += 0.03
                begin = max(now, free.get(i["link"], 0.0))
                free[i["link"]] = begin + i["size"] * i["hops"] / rate
                arrivals[n] = free[i["link"]] + hop + 0.3 * (i["hops"] - 1)
                started.add(n)
                steps.append(("start", n))
            if arrivals:
                first = min(arrivals, key=lambda n: (arrivals[n], n))
                if arrivals[first] <= now:
                    steps.append(("wait", first))
                    arrivals.pop(first)
                    done.add(first)
                    now += 0.02
                    continue
            runs = sorted((n for n in ready if self.items[n]["kind"] == "c"), key=lambda n: self.items[n]["rank"])
            if runs:
                n = runs[0]
                now += self.items[n]["cost"]
                started.add(n)
                done.add(n)
                steps.append(("run", n))
                continue
            first = min(arrivals, key=lambda n: (arrivals[n], n))
            now = max(now, arrivals.pop(first)) + 0.02
            steps.append(("wait", first))
            done.add(first)
        self.end = now
        return steps


def kernel(q_ref, g_ref, k_hbm, v_hbm, qg_ref, kg_hbm, vg_hbm,
           blocks, rows, kv, norm, spread, gather_rows, probs, dscores, scores, dprobs,
           stat_y, stat_x, stat_f, rs, rs_x, rs_t, rs_y, rs_z, own, cross_out, cross_in, outs,
           send_sem, recv_sem, cross_send, cross_recv, load_sem, store_sem):
    dp = lax.axis_index("dp")
    slot = lax.axis_index("slot")
    c = slot % 2
    y = (slot // 2) % NY
    zh = (slot // 16) % 2
    x = slot // 32
    z = zh * NDP + dp

    def chip(dx, dy, dz):
        zz = (z + dz + NZ) % NZ
        return {"dp": zz % NDP, "slot": ((((x + dx + NX) % NX) * 2 + zz // NDP) * NY + (y + dy + NY) % NY) * 2 + c}

    other_core = {"dp": dp, "slot": slot + 1 - 2 * c}

    loads = []
    for n, src in enumerate((k_hbm, v_hbm)):
        cp = pltpu.make_async_copy(src, kv.at[n, c], load_sem.at[n])
        cp.start()
        loads.append(cp)

    barrier = pltpu.get_barrier_semaphore()
    peers = [chip(d, 0, 0) for d in range(1, NX)] + [chip(0, d, 0) for d in range(1, NY)]
    peers += [chip(0, 0, d) for d in range(1, NZ)] + [chip(d, 0, 4) for d in range(1, NX)] + [other_core]
    for p in peers:
        pl.semaphore_signal(barrier, inc=1, device_id=p, device_id_type=MESH)

    def to_rows16(ref):
        wide = ref[...].astype(F32)
        return jnp.concatenate([wide[r:r + 1, i * F:(i + 1) * F] for r in range(2) for i in range(NF)], axis=0).astype(BF)

    blocks[z, 0, x, y] = to_rows16(q_ref)
    blocks[z, 1, x, y] = to_rows16(g_ref)

    row = lax.broadcasted_iota(jnp.int32, (256, 256), 0)
    col = lax.broadcasted_iota(jnp.int32, (256, 256), 1)
    spread[...] = jnp.where(col == (row % 32) * NF + row // 32, 1.0, 0.0).astype(BF)
    want = (row % 8) * 32 + ((row // 16) % 2) * 16 + (row // 32) * 2 + (row // 8) % 2
    gather_rows[...] = jnp.where(col == want, 1.0, 0.0).astype(BF)

    pl.semaphore_wait(barrier, len(peers))

    plan = Plan()
    emit = {}
    index = {}

    def transfer(name, needs, link, size, src, dst, incoming, peer, hops=1, rank=0):
        n = index.setdefault(name, len(index))
        plan.transfer(name, needs, link, size, hops, rank)

        def out():
            return pltpu.make_async_remote_copy(
                src_ref=src(), dst_ref=dst(), send_sem=send_sem.at[n], recv_sem=recv_sem.at[n],
                device_id=peer, device_id_type=MESH)

        def into():
            return pltpu.make_async_remote_copy(
                src_ref=incoming(), dst_ref=incoming(), send_sem=send_sem.at[n], recv_sem=recv_sem.at[n],
                device_id=peer, device_id_type=MESH)

        emit[name] = (out, into)

    def compute(name, needs, cost, run, rank=0):
        plan.compute(name, needs, cost, rank)
        emit[name] = run

    def at(dz, a, dx, dy):
        xs = dx if not isinstance(dx, int) else (x + dx + NX) % NX
        ys = dy if not isinstance(dy, int) else (y + dy + NY) % NY
        return blocks.at[(z + dz + NZ) % NZ, a, xs, ys]

    def move(name, needs, link, size, dz, a, dx, dy, step, hops=1, rank=0):
        ex, ey, ez = step

        def shifted(d, e):
            return d if not isinstance(d, int) else d - e

        transfer(name, needs, link, size, lambda: at(dz, a, dx, dy), lambda: at(dz, a, dx, dy),
                 lambda: at(dz - ez, a, shifted(dx, ex), shifted(dy, ey)), chip(*step), hops, rank)

    KIB = 1024
    every = slice(None)

    for ez in (4, 3, -3, 2, -2):
        move(f"z1 {ez}", [], "z+" if ez > 0 else "z-", 32 * KIB, 0, every, 0, 0, (0, 0, ez), hops=abs(ez),
             rank=PLANE.index(ez if ez == 4 else -ez))

    arrived = {(dz, a): [] for dz in range(-3, 5) for a in range(2)}
    for u, dz in enumerate(PLANE):
        have = [] if dz == 0 else [f"z1 {4 if dz == 4 else -dz}"]
        firsts = []
        for e in (1, -1, 2):
            name = f"xp {dz} {e}"
            move(name, have, "x-" if e < 0 else "x+", 16 * KIB, dz, 0, 0, 0, (e, 0, 0), hops=abs(e), rank=u)
            firsts.append(name)
        for way in (1, -1):
            for k in range(4):
                needs = firsts + have if k == 0 else [f"yl {dz} {way} {k - 1}"]
                half = every if k < 3 else (pl.ds(0, 2) if way > 0 else pl.ds(2, 2))
                move(f"yl {dz} {way} {k}", needs, "y+" if way > 0 else "y-", (64 if k < 3 else 32) * KIB,
                     dz, 0, half, -way * k, (0, way, 0), rank=u + 0.5)
        arrived[dz, 0] += firsts + [f"yl {dz} {way} {k}" for way in (1, -1) for k in range(4)]
        firsts = []
        for way in (1, -1):
            for k in range(4 if (way > 0) == (u % 2 == 0) else 3):
                name = f"yp {dz} {way} {k}"
                needs = have if k == 0 else [f"yp {dz} {way} {k - 1}"]
                move(name, needs, "y+" if way > 0 else "y-", 16 * KIB, dz, 1, 0, -way * k, (0, way, 0), rank=u)
                firsts.append(name)
        for e in (1, -1):
            move(f"xl {dz} {e} 0", firsts + have, "x+" if e > 0 else "x-", 128 * KIB, dz, 1, 0, every, (e, 0, 0), rank=u + 0.5)
            move(f"xl {dz} {e} 1", [f"xl {dz} {e} 0"], "x+" if e > 0 else "x-", 64 * KIB, dz, 1, -e,
                 pl.ds(0, 4) if e > 0 else pl.ds(4, 4), (e, 0, 0), rank=u + 0.5)
        arrived[dz, 1] += firsts + [f"xl {dz} {e} {k}" for e in (1, -1) for k in range(2)]

    for ez in (1, -1):
        link = "z+" if ez > 0 else "z-"
        name = f"zq {ez} own"
        move(name, [f"xp 0 {e}" for e in (1, -1, 2)], link, 64 * KIB, 0, 0, every, 0, (0, 0, ez), rank=3)
        arrived[-ez, 0].append(name)
        name = f"zg {ez} own"
        move(name, [f"yp 0 {w} {k}" for w in (1, -1) for k in range(4 if w > 0 else 3)], link, 128 * KIB,
             0, 1, 0, every, (0, 0, ez), rank=3)
        arrived[-ez, 1].append(name)
        for way in (1, -1):
            for k in range(4):
                half = every if k < 3 else (pl.ds(0, 2) if way > 0 else pl.ds(2, 2))
                name = f"zq {ez} {way} {k}"
                move(name, [f"yl 0 {way} {k}"], link, (64 if k < 3 else 32) * KIB, 0, 0, half, -way * (k + 1), (0, 0, ez), rank=3)
                arrived[-ez, 0].append(name)
            for k in range(2):
                half = every if k < 1 else (pl.ds(0, 4) if way > 0 else pl.ds(4, 4))
                name = f"zg {ez} {way} {k}"
                move(name, [f"xl 0 {way} {k}"], link, (128 if k < 1 else 64) * KIB, 0, 1, -way * (k + 1), half, (0, 0, ez), rank=3)
                arrived[-ez, 1].append(name)

    def load(n):
        return lambda: loads[n].wait()

    for n in range(2):
        compute(f"load {n}", [], 0.6, load(n), rank=5)
        transfer(f"kv {n}", [f"load {n}"], "core", 1280 * KIB, lambda n=n: kv.at[n, c], lambda n=n: kv.at[n, c],
                 lambda n=n: kv.at[n, 1 - c], other_core, rank=9)

    def key_norm():
        for half in range(2):
            def add(i, total):
                part = kv[0, half, :, pl.ds(pl.multiple_of(i * 128, 128), 128)].astype(F32)
                return total + part * part
            total = lax.fori_loop(0, D // 128, add, jnp.zeros((SL, 128), F32))
            norm[pl.ds(half * SL, SL), :] = jnp.broadcast_to(
                (0.5 * BETA) * jnp.sum(total, axis=1, keepdims=True), (SL, 128))

    compute("norm", ["load 0", "kv 0"], 1.5, key_norm, rank=6)

    def relayout(dz, a):
        def run():
            zz = (z + dz + NZ) % NZ
            for h in range(2):
                got = blocks[zz, a, 2 * h:2 * h + 2].reshape(256, F)
                laid = jnp.dot(spread[...], got, preferred_element_type=F32).astype(BF)
                for i in range(NF):
                    rows[a, zz % NDP, zz // NDP, pl.ds(32 * h, 32), i * F:(i + 1) * F] = laid[i * 32:(i + 1) * 32]
        return run

    for dz in range(-3, 5):
        for a in range(2):
            needs = arrived[dz, a] + ([] if dz in (0, 1, -1) else [f"z1 {4 if dz == 4 else -dz}"])
            compute(f"rows {dz} {a}", needs, 0.35, relayout(dz, a), rank=3 if dz in (0, 4) else 8)

    def products(group):
        def one(n):
            def add(i, total):
                cut = pl.ds(pl.multiple_of(i * 1024, 1024), 1024)
                left = kv[n, :, :, cut].reshape(2 * SL, 1024)
                right = rows[n, group, :, :, cut].reshape(128, 1024)
                return total + lax.dot_general(left, right, (((1,), (1,)), ((), ())), preferred_element_type=F32)
            return lax.fori_loop(0, D // 1024, add, jnp.zeros((2 * SL, 128), F32))
        return BETA * one(0) - norm[...], one(1)

    def own_scores():
        s, d = products(dp)
        scores[...] = s
        dprobs[...] = d
        top = jnp.max(s, axis=0, keepdims=True)
        e = jnp.exp(s - top)
        stat_y[y, 0:1] = top
        stat_y[y, 1:2] = jnp.sum(e, axis=0, keepdims=True)
        stat_y[y, 2:3] = jnp.sum(e * d, axis=0, keepdims=True)
        stat_y[y, 3:8] = jnp.zeros((5, 128), F32)

    def merge(ref):
        parts = [ref[i] for i in range(8)]
        top = parts[0][0:1]
        for p in parts[1:]:
            top = jnp.maximum(top, p[0:1])
        total = jnp.zeros((1, 128), F32)
        weighted = jnp.zeros((1, 128), F32)
        for p in parts:
            scale = jnp.exp(p[0:1] - top)
            total += p[1:2] * scale
            weighted += p[2:3] * scale
        return top, total, weighted

    compute("own scores", ["rows 0 0", "rows 0 1", "rows 4 0", "rows 4 1", "norm", "load 1", "kv 1"], 1.6, own_scores, rank=1)
    for d in range(1, NY):
        transfer(f"sy {d}", ["own scores"], f"sy{d}", 4 * KIB, lambda: stat_y.at[y], lambda: stat_y.at[y],
                 lambda d=d: stat_y.at[(y - d + NY) % NY], chip(0, d, 0), rank=-5)

    place = x * 2 + zh

    def merge_y():
        top, total, weighted = merge(stat_y)
        stat_x[place, 0:1] = top
        stat_x[place, 1:2] = total
        stat_x[place, 2:3] = weighted
        stat_x[place, 3:8] = jnp.zeros((5, 128), F32)

    compute("merge y", [f"sy {d}" for d in range(1, NY)], 0.3, merge_y, rank=0)
    for d in range(NX):
        for e in range(2):
            if d or e:
                transfer(f"sx {d} {e}", ["merge y"], f"sx{d}{e}", 4 * KIB, lambda: stat_x.at[place], lambda: stat_x.at[place],
                         lambda d=d, e=e: stat_x.at[((x - d + NX) % NX) * 2 + (zh + e) % 2], chip(d, 0, 4 * e), rank=-5)

    def merge_x():
        top, total, weighted = merge(stat_x)
        stat_f[dp, 0:1] = top + jnp.log(total)
        stat_f[dp, 1:2] = weighted / total
        stat_f[dp, 2:8] = jnp.zeros((6, 128), F32)

    compute("merge x", [f"sx {d} {e}" for d in range(NX) for e in range(2) if d or e], 0.3, merge_x, rank=0)
    for d in range(1, NDP):
        transfer(f"sf {d}", ["merge x"], f"sf{d}", 4 * KIB, lambda: stat_f.at[dp], lambda: stat_f.at[dp],
                 lambda d=d: stat_f.at[(dp - d + NDP) % NDP], {"dp": (dp + d) % NDP, "slot": slot}, rank=-5)

    def weights(group, s, d):
        lse = stat_f[group, 0:1]
        delta = stat_f[group, 1:2]
        prob = jnp.exp(s - lse)
        dscore = (BETA * prob * (d - delta)).astype(BF)
        probs[group] = prob.astype(BF).reshape(2, SL, 128)
        dscores[group] = dscore.reshape(2, SL, 128)
        return dscore

    def own_weights():
        dscore = weights(dp, scores[...], dprobs[...])
        turned = dscore.astype(F32).T.astype(BF)

        def part(i, _):
            cut = pl.ds(pl.multiple_of(i * F, F), F)
            out = jnp.dot(turned, kv[0, :, :, cut].reshape(2 * SL, F), preferred_element_type=F32)
            rs[:, :, :, cut] = out.astype(BF).reshape(2, NX, 16, F)
            return 0
        lax.fori_loop(0, NF, part, 0)

    compute("own weights", ["merge x"], 1.5, own_weights, rank=0)
    for d in range(1, NX):
        transfer(f"rx {d}", ["own weights"], "x-" if d == 3 else "x+", 256 * KIB, lambda d=d: rs.at[:, (x + d) % NX],
                 lambda d=d: rs_x.at[d - 1], lambda d=d: rs_x.at[d - 1], chip(d, 0, 0), hops=2 if d == 2 else 1, rank=-2)

    def reduce_x():
        for i in range(NF):
            cut = slice(i * F, (i + 1) * F)
            total = rs[:, x, :, cut].astype(F32)
            for d in range(NX - 1):
                total += rs_x[d, :, :, cut].astype(F32)
            rs_t[pl.ds(32 * i, 32), :] = total.reshape(32, F).astype(BF)
        laid = jnp.dot(gather_rows[...], rs_t[...], preferred_element_type=F32).astype(BF)
        rs_t[...] = laid

    compute("reduce x", [f"rx {d}" for d in range(1, NX)], 0.6, reduce_x, rank=0)
    for d in range(1, NY):
        transfer(f"ry {d}", ["reduce x"], "y+" if d <= 4 else "y-", 32 * KIB,
                 lambda d=d: rs_t.at[pl.ds(pl.multiple_of(((y + d) % NY) * 32, 32), 32)],
                 lambda d=d: rs_y.at[d - 1], lambda d=d: rs_y.at[d - 1], chip(0, d, 0), hops=min(d, NY - d), rank=-3)

    def reduce_y():
        total = rs_t[pl.ds(pl.multiple_of(y * 32, 32), 32), :].astype(F32)
        for d in range(NY - 1):
            total += rs_y[d].astype(F32)
        rs_z[0:2] = total.astype(BF).reshape(2, 16, F)

    compute("reduce y", [f"ry {d}" for d in range(1, NY)], 0.3, reduce_y, rank=0)
    transfer("rz", ["reduce y"], "z+", 16 * KIB, lambda: rs_z.at[1 - zh], lambda: rs_z.at[2], lambda: rs_z.at[2],
             chip(0, 0, 4), hops=4, rank=-3)

    def finish_queries():
        total = rs_z[zh].astype(F32) + rs_z[2].astype(F32)
        lines = [jnp.concatenate([total[8 * r + i:8 * r + i + 1] for i in range(NF)], axis=1) for r in range(2)]
        qg_ref[...] = jnp.concatenate(lines, axis=0).astype(BF)

    compute("finish queries", ["rz"], 0.2, finish_queries, rank=12)

    def other_group(k):
        def run():
            group = (dp + k) % NDP
            s, d = products(group)
            weights(group, s, d)
        return run

    for k in range(1, NDP):
        zs = [k, k - 4]
        compute(f"group {k}", [f"rows {d} {a}" for d in zs for a in range(2)] + [f"sf {NDP - k}", "norm", "load 1", "kv 1"],
                1.6, other_group(k), rank=7)

    assert len(index) <= TRANSFERS
    for what, name in plan.order():
        if what == "start":
            emit[name][0]().start()
        elif what == "wait":
            emit[name][1]().wait_recv()
        else:
            emit[name]()

    def gradients(core, store):
        left_k = jnp.concatenate([dscores[i, core] for i in range(NDP)], axis=1)
        left_v = jnp.concatenate([probs[i, core] for i in range(NDP)], axis=1)
        column = jnp.sum(left_k.astype(F32), axis=1, keepdims=True)

        def part(i, _):
            cut = pl.ds(pl.multiple_of(i * F, F), F)
            grad = jnp.dot(left_k, rows[0, :, :, :, cut].reshape(512, F), preferred_element_type=F32)
            grad -= column * kv[0, core, :, cut].astype(F32)
            store(i, 0, grad)
            store(i, 1, jnp.dot(left_v, rows[1, :, :, :, cut].reshape(512, F), preferred_element_type=F32))
            return 0
        lax.fori_loop(0, NF, part, 0)

    def crossing(i):
        return pltpu.make_async_remote_copy(
            src_ref=cross_out.at[i], dst_ref=cross_in.at[i], send_sem=cross_send.at[i], recv_sem=cross_recv.at[i],
            device_id=other_core, device_id_type=MESH)

    def store_out(i, n, value):
        cross_out[i, n] = value.astype(BF)
        if n == 1:
            crossing(i).start()

    def store_own(i, n, value):
        own[i, n] = value

    gradients(1 - c, store_out)
    gradients(c, store_own)

    def storing(i, n, ref):
        cut = pl.ds(pl.multiple_of(i * F, F), F)
        return pltpu.make_async_copy(outs.at[i, n], ref.at[:, cut], store_sem.at[i, n])

    def finish(i, _):
        crossing(i).wait()
        for n, ref in enumerate((kg_hbm, vg_hbm)):
            outs[i, n] = (own[i, n] + cross_in[i, n].astype(F32)).astype(BF)
            storing(i, n, ref).start()
        return 0
    lax.fori_loop(0, NF, finish, 0)

    for name, n in index.items():
        emit[name][0]().wait_send()
    for i in range(NF):
        for n, ref in enumerate((kg_hbm, vg_hbm)):
            storing(i, n, ref).wait()


TRANSFERS = 200


def body(queries, keys, values, cotangent):
    vmem = pl.BlockSpec(memory_space=pltpu.VMEM)
    hbm = pl.BlockSpec(memory_space=pl.ANY)
    grads = pl.pallas_call(
        kernel,
        name="memory_backward",
        out_shape=(
            jax.ShapeDtypeStruct((2, D), BF),
            jax.ShapeDtypeStruct((SL, D), BF),
            jax.ShapeDtypeStruct((SL, D), BF),
        ),
        in_specs=[vmem, vmem, hbm, hbm],
        out_specs=(vmem, hbm, hbm),
        scratch_shapes=[
            pltpu.VMEM((NZ, 2, NX, NY, 16, F), BF),
            pltpu.VMEM((2, NDP, 2, 64, D), BF),
            pltpu.VMEM((2, 2, SL, D), BF),
            pltpu.VMEM((2 * SL, 128), F32),
            pltpu.VMEM((256, 256), BF),
            pltpu.VMEM((256, 256), BF),
            pltpu.VMEM((NDP, 2, SL, 128), BF),
            pltpu.VMEM((NDP, 2, SL, 128), BF),
            pltpu.VMEM((2 * SL, 128), F32),
            pltpu.VMEM((2 * SL, 128), F32),
            pltpu.VMEM((NY, 8, 128), F32),
            pltpu.VMEM((2 * NX, 8, 128), F32),
            pltpu.VMEM((NDP, 8, 128), F32),
            pltpu.VMEM((2, NX, 16, D), BF),
            pltpu.VMEM((NX - 1, 2, 16, D), BF),
            pltpu.VMEM((256, F), BF),
            pltpu.VMEM((NY - 1, 32, F), BF),
            pltpu.VMEM((3, 16, F), BF),
            pltpu.VMEM((NF, 2, SL, F), F32),
            pltpu.VMEM((NF, 2, SL, F), BF),
            pltpu.VMEM((NF, 2, SL, F), BF),
            pltpu.VMEM((NF, 2, SL, F), BF),
            pltpu.SemaphoreType.DMA((TRANSFERS,)),
            pltpu.SemaphoreType.DMA((TRANSFERS,)),
            pltpu.SemaphoreType.DMA((NF,)),
            pltpu.SemaphoreType.DMA((NF,)),
            pltpu.SemaphoreType.DMA((2,)),
            pltpu.SemaphoreType.DMA((NF, 2)),
        ],
        compiler_params=pltpu.CompilerParams(
            collective_id=0, has_side_effects=True, vmem_limit_bytes=56 * 2**20
        ),
    )(queries, cotangent, keys, values)
    return grads


def solution(mesh):
    rows = P(("dp", "slot"), None)
    slots = P("slot", None)
    return jax.shard_map(
        body,
        mesh=mesh,
        in_specs=(rows, slots, slots, rows),
        out_specs=(rows, slots, slots),
        check_vma=False,
    )
```

```python
import jax
import jax.numpy as jnp
from jax import lax
from jax.experimental import pallas as pl
from jax.experimental.pallas import tpu as pltpu
from jax.sharding import PartitionSpec as P

MESH = pl.DeviceIdType.MESH
D = 4096
BETA = 1.25 * D ** (-0.5)
NX, NY, NZ, NDP = 4, 8, 8, 4
SL = 160
F = 512
NF = D // F
BF = jnp.bfloat16
F32 = jnp.float32


UNITS = ((0, 0), (0, 1), (4, 0), (4, 1), (3, 0), (3, 1), (-3, 0), (-3, 1), (2, 0), (-2, 1))

HOP_US = 1.9
CORE_HOP_US = 1.5
LINK_RATE = 48e3
CORE_RATE = 500e3
BACKLOG_US = 1.0
FIRST_RANK = 0.5
START_US = 0.03
WAIT_US = 0.02


class Plan:
    def __init__(self):
        self.items = {}

    def transfer(self, name, needs, link, size, hops=1, rank=0):
        self.items[name] = dict(kind="t", needs=list(needs), link=link, size=size, hops=hops, rank=rank)

    def compute(self, name, needs, cost, rank=0):
        self.items[name] = dict(kind="c", needs=list(needs), cost=cost, rank=rank)

    def order(self):
        now = 0.0
        done, started, arrivals, free, steps = set(), set(), {}, {}, []
        while len(done) < len(self.items):
            ready = [
                n for n, i in self.items.items()
                if n not in started and all(d in done for d in i["needs"])
            ]
            held = []
            sends = sorted((n for n in ready if self.items[n]["kind"] == "t"), key=lambda n: self.items[n]["rank"])
            for n in sends:
                i = self.items[n]
                rate, hop = (CORE_RATE, CORE_HOP_US) if i["link"] == "core" else (LINK_RATE, HOP_US)
                links = [i["link"][0] + w for w in "+-"] if i["link"].endswith("*") else [i["link"]]
                queued = max(free.get(link, 0.0) for link in links)
                if queued - now > BACKLOG_US and i["rank"] > 0:
                    held.append(queued - BACKLOG_US)
                    continue
                now += START_US
                for link in links:
                    free[link] = max(now, free.get(link, 0.0)) + i["size"] * i["hops"] / rate / len(links)
                arrivals[n] = max(free[link] for link in links) + hop + 0.3 * (i["hops"] - 1)
                started.add(n)
                steps.append(("start", n))
            first = min(arrivals, key=lambda n: (arrivals[n], n)) if arrivals else None
            if first is not None and arrivals[first] <= now:
                steps.append(("wait", first))
                arrivals.pop(first)
                done.add(first)
                now += WAIT_US
                continue
            runs = sorted((n for n in ready if self.items[n]["kind"] == "c"), key=lambda n: self.items[n]["rank"])
            if runs:
                n = runs[0]
                now += self.items[n]["cost"]
                started.add(n)
                done.add(n)
                steps.append(("run", n))
                continue
            if held and (first is None or min(held) < arrivals[first]):
                now = max(now, min(held)) + 0.001
                continue
            now = max(now, arrivals.pop(first)) + WAIT_US
            steps.append(("wait", first))
            done.add(first)
        self.end = now
        return steps


def kernel(q_ref, g_ref, k_hbm, v_hbm, qg_ref, kg_hbm, vg_hbm,
           blocks, rows, kv, norm, spread, gather_rows, turned, probs, dscores, scores, dprobs,
           stat_y, stat_x, stat_f, rs, rs_a, rs_x, rs_t, rs_y, rs_z, own, cross_out, cross_in, outs,
           send_sem, recv_sem, load_sem, store_sem):
    dp = lax.axis_index("dp")
    slot = lax.axis_index("slot")
    c = slot % 2
    y = (slot // 2) % NY
    zh = (slot // 16) % 2
    x = slot // 32
    z = zh * NDP + dp

    def chip(dx, dy, dz):
        zz = (z + dz + NZ) % NZ
        return {"dp": zz % NDP, "slot": ((((x + dx + NX) % NX) * 2 + zz // NDP) * NY + (y + dy + NY) % NY) * 2 + c}

    other_core = {"dp": dp, "slot": slot + 1 - 2 * c}

    loads = []
    for n, src in enumerate((k_hbm, v_hbm)):
        cp = pltpu.make_async_copy(src, kv.at[n, c], load_sem.at[n])
        cp.start()
        loads.append(cp)

    barrier = pltpu.get_barrier_semaphore()
    peers = [chip(d, 0, 0) for d in range(1, NX)] + [chip(0, d, 0) for d in range(1, NY)]
    peers += [chip(0, 0, d) for d in range(1, NZ)] + [chip(d, 0, 4) for d in range(1, NX)] + [other_core]
    for p in peers:
        pl.semaphore_signal(barrier, inc=1, device_id=p, device_id_type=MESH)

    def to_rows16(ref):
        wide = ref[...].astype(F32)
        return jnp.concatenate([wide[r:r + 1, i * F:(i + 1) * F] for r in range(2) for i in range(NF)], axis=0).astype(BF)

    blocks[z, 0, x, y] = to_rows16(q_ref)
    blocks[z, 1, x, y] = to_rows16(g_ref)

    row = lax.broadcasted_iota(jnp.int32, (256, 256), 0)
    col = lax.broadcasted_iota(jnp.int32, (256, 256), 1)
    spread[...] = jnp.where(col == (row % 32) * NF + row // 32, 1.0, 0.0).astype(BF)
    want = (row % 8) * 32 + ((row // 16) % 2) * 16 + (row // 32) * 2 + (row // 8) % 2
    gather_rows[...] = jnp.where(col == want, 1.0, 0.0).astype(BF)

    pl.semaphore_wait(barrier, len(peers))

    plan = Plan()
    emit = {}
    index = {}

    def transfer(name, needs, link, size, src, dst, incoming, peer, hops=1, rank=0):
        n = index.setdefault(name, len(index))
        plan.transfer(name, needs, link, size, hops, rank)

        def out():
            return pltpu.make_async_remote_copy(
                src_ref=src(), dst_ref=dst(), send_sem=send_sem.at[n], recv_sem=recv_sem.at[n],
                device_id=peer, device_id_type=MESH)

        def into():
            return pltpu.make_async_remote_copy(
                src_ref=incoming(), dst_ref=incoming(), send_sem=send_sem.at[n], recv_sem=recv_sem.at[n],
                device_id=peer, device_id_type=MESH)

        emit[name] = (out, into)

    def compute(name, needs, cost, run, rank=0):
        plan.compute(name, needs, cost, rank)
        emit[name] = run

    def at(dz, a, dx, dy):
        xs = dx if not isinstance(dx, int) else (x + dx + NX) % NX
        ys = dy if not isinstance(dy, int) else (y + dy + NY) % NY
        return blocks.at[(z + dz + NZ) % NZ, a, xs, ys]

    def move(name, needs, link, size, dz, a, dx, dy, step, hops=1, rank=0):
        ex, ey, ez = step

        def shifted(d, e):
            return d if not isinstance(d, int) else d - e

        transfer(name, needs, link, size, lambda: at(dz, a, dx, dy), lambda: at(dz, a, dx, dy),
                 lambda: at(dz - ez, a, shifted(dx, ex), shifted(dy, ey)), chip(*step), hops, rank)

    KIB = 1024
    every = slice(None)

    for ez, a in ((4, 0), (4, 1), (-3, 0), (3, 0), (-3, 1), (3, 1), (-2, 0), (2, 1)):
        move(f"z1 {ez} {a}", [], "z*" if ez == 4 else "z+" if ez > 0 else "z-", 16 * KIB, 0, a, 0, 0, (0, 0, ez),
             hops=abs(ez), rank=0 if ez == 4 else FIRST_RANK)

    def first_hop(dz, a):
        return [] if dz == 0 else [f"z1 4 {a}" if dz == 4 else f"z1 {-dz} {a}"]

    def line_parts(dz):
        return (0, 1) if dz in (0, 4) else (None,)

    arrived = {(dz, a): [] for dz in range(-3, 5) for a in range(2)}
    for u, (dz, a) in enumerate(UNITS):
        have = first_hop(dz, a)
        near = dz in (0, 4)
        rank = 0 if near else u
        firsts = []
        if a == 0:
            for e in (1, -1, 2):
                name = f"xp {dz} {e}"
                move(name, have, "x*" if e == 2 else "x-" if e < 0 else "x+", 16 * KIB, dz, 0, 0, 0, (e, 0, 0), hops=abs(e), rank=min(rank, FIRST_RANK))
                firsts.append(name)
            for k in range(4):
                for way in (1, -1):
                    for h in line_parts(dz):
                        if k == 3 and h == (1 if way > 0 else 0):
                            continue
                        needs = firsts + have if k == 0 else [f"yl {dz} {way} {k - 1} {h}"]
                        half = (pl.ds(0, 2) if way > 0 else pl.ds(2, 2)) if k == 3 else every if h is None else pl.ds(2 * h, 2)
                        name = f"yl {dz} {way} {k} {h}"
                        move(name, needs, "y+" if way > 0 else "y-", (64 if k < 3 and h is None else 32) * KIB,
                             dz, 0, half, -way * k, (0, way, 0), rank=rank)
                        arrived[dz, 0].append(name)
        else:
            if near:
                for d in range(1, NY):
                    name = f"yp {dz} {d}"
                    move(name, have, "y*" if d == 4 else "y+" if d < 4 else "y-", 16 * KIB, dz, 1, 0, 0, (0, d, 0), hops=min(d, NY - d), rank=min(rank, FIRST_RANK))
                    firsts.append(name)
            else:
                for way in (1, -1):
                    for k in range(4 if (way > 0) == (u % 4 == 1) else 3):
                        name = f"yp {dz} {way} {k}"
                        needs = have if k == 0 else [f"yp {dz} {way} {k - 1}"]
                        move(name, needs, "y+" if way > 0 else "y-", 16 * KIB, dz, 1, 0, -way * k, (0, way, 0), rank=min(rank, FIRST_RANK))
                        firsts.append(name)
            for e in (1, -1):
                for k in range(2):
                    needs = firsts + have if k == 0 else [f"xl {dz} {e} 0"]
                    name = f"xl {dz} {e} {k}"
                    half = every if k == 0 else (pl.ds(0, 4) if e > 0 else pl.ds(4, 4))
                    move(name, needs, "x+" if e > 0 else "x-", (128 if k == 0 else 64) * KIB, dz, 1, -e * k, half,
                         (e, 0, 0), rank=rank)
                    arrived[dz, 1].append(name)
        arrived[dz, a] += firsts + have
        if dz == 0:
            own_line = (firsts if a == 0 else own_line[0], firsts)

    for ez in (1, -1):
        link = "z+" if ez > 0 else "z-"
        lines = [(0, "own", own_line[0], 64, every, 0), (1, "own", own_line[1], 128, 0, every)]
        for way in (1, -1):
            for k in range(4):
                half = every if k < 3 else (pl.ds(0, 2) if way > 0 else pl.ds(2, 2))
                needs = [n for n in arrived[0, 0] if n.startswith(f"yl 0 {way} {k}")]
                lines.append((0, f"{way} {k}", needs, 64 if k < 3 else 32, half, -way * (k + 1)))
            for k in range(2):
                half = every if k < 1 else (pl.ds(0, 4) if way > 0 else pl.ds(4, 4))
                lines.append((1, f"{way} {k}", [f"xl 0 {way} {k}"], 128 if k < 1 else 64, -way * (k + 1), half))
        for a, label, needs, size, dx, dy in lines:
            name = f"zl {a} {ez} {label}"
            move(name, needs, link, size * KIB, 0, a, dx, dy, (0, 0, ez), rank=3)
            arrived[-ez, a].append(name)
            if a == (0 if ez > 0 else 1):
                further = f"zf {a} {ez} {label}"
                move(further, [name], link, size * KIB, -ez, a, dx, dy, (0, 0, ez), rank=4)
                arrived[-2 * ez, a].append(further)

    def load(n):
        return lambda: loads[n].wait()

    for n in range(2):
        compute(f"load {n}", [], 0.6, load(n), rank=5)
        transfer(f"kv {n}", [f"load {n}"], "core", 1280 * KIB, lambda n=n: kv.at[n, c], lambda n=n: kv.at[n, c],
                 lambda n=n: kv.at[n, 1 - c], other_core, rank=9)

    def key_norm():
        for half in range(2):
            def add(i, total):
                part = kv[0, half, :, pl.ds(pl.multiple_of(i * 128, 128), 128)].astype(F32)
                return total + part * part
            total = lax.fori_loop(0, D // 128, add, jnp.zeros((SL, 128), F32))
            norm[pl.ds(half * SL, SL), :] = jnp.broadcast_to(
                (0.5 * BETA) * jnp.sum(total, axis=1, keepdims=True), (SL, 128))

    compute("norm", ["load 0", "kv 0"], 1.5, key_norm, rank=6)

    def relayout(dz, a):
        def run():
            zz = (z + dz + NZ) % NZ
            for h in range(2):
                got = blocks[zz, a, 2 * h:2 * h + 2].reshape(256, F)
                laid = jnp.dot(spread[...], got, preferred_element_type=F32).astype(BF)
                for i in range(NF):
                    rows[a, zz % NDP, zz // NDP, pl.ds(32 * h, 32), i * F:(i + 1) * F] = laid[i * 32:(i + 1) * 32]
        return run

    for dz in range(-3, 5):
        for a in range(2):
            compute(f"rows {dz} {a}", arrived[dz, a], 0.35, relayout(dz, a), rank=3 if dz in (0, 4) else 8)

    def products(group):
        def one(n):
            def add(i, total):
                cut = pl.ds(pl.multiple_of(i * 1024, 1024), 1024)
                left = kv[n, :, :, cut].reshape(2 * SL, 1024)
                right = rows[n, group, :, :, cut].reshape(128, 1024)
                return total + lax.dot_general(left, right, (((1,), (1,)), ((), ())), preferred_element_type=F32)
            return lax.fori_loop(0, D // 1024, add, jnp.zeros((2 * SL, 128), F32))
        return BETA * one(0) - norm[...], one(1)

    def own_scores():
        s, d = products(dp)
        scores[...] = s
        dprobs[...] = d
        top = jnp.max(s, axis=0, keepdims=True)
        e = jnp.exp(s - top)
        stat_y[y, 0:1] = top
        stat_y[y, 1:2] = jnp.sum(e, axis=0, keepdims=True)
        stat_y[y, 2:3] = jnp.sum(e * d, axis=0, keepdims=True)
        stat_y[y, 3:8] = jnp.zeros((5, 128), F32)

    def merge(ref):
        parts = [ref[i] for i in range(8)]
        top = parts[0][0:1]
        for p in parts[1:]:
            top = jnp.maximum(top, p[0:1])
        total = jnp.zeros((1, 128), F32)
        weighted = jnp.zeros((1, 128), F32)
        for p in parts:
            scale = jnp.exp(p[0:1] - top)
            total += p[1:2] * scale
            weighted += p[2:3] * scale
        return top, total, weighted

    compute("own scores", ["rows 0 0", "rows 0 1", "rows 4 0", "rows 4 1", "norm", "load 1", "kv 1"], 1.6, own_scores, rank=1)
    for d in range(1, NY):
        transfer(f"sy {d}", ["own scores"], f"sy{d}", 4 * KIB, lambda: stat_y.at[y], lambda: stat_y.at[y],
                 lambda d=d: stat_y.at[(y - d + NY) % NY], chip(0, d, 0), rank=-5)

    place = x * 2 + zh

    def merge_y():
        top, total, weighted = merge(stat_y)
        stat_x[place, 0:1] = top
        stat_x[place, 1:2] = total
        stat_x[place, 2:3] = weighted
        stat_x[place, 3:8] = jnp.zeros((5, 128), F32)

    compute("merge y", [f"sy {d}" for d in range(1, NY)], 0.3, merge_y, rank=0)
    for d in range(NX):
        for e in range(2):
            if d or e:
                transfer(f"sx {d} {e}", ["merge y"], f"sx{d}{e}", 4 * KIB, lambda: stat_x.at[place], lambda: stat_x.at[place],
                         lambda d=d, e=e: stat_x.at[((x - d + NX) % NX) * 2 + (zh + e) % 2], chip(d, 0, 4 * e), rank=-5)

    def merge_x():
        top, total, weighted = merge(stat_x)
        stat_f[dp, 0:1] = top + jnp.log(total)
        stat_f[dp, 1:2] = weighted / total
        stat_f[dp, 2:8] = jnp.zeros((6, 128), F32)

    compute("merge x", [f"sx {d} {e}" for d in range(NX) for e in range(2) if d or e], 0.3, merge_x, rank=0)
    for d in range(1, NDP):
        transfer(f"sf {d}", ["merge x"], f"sf{d}", 4 * KIB, lambda: stat_f.at[dp], lambda: stat_f.at[dp],
                 lambda d=d: stat_f.at[(dp - d + NDP) % NDP], {"dp": (dp + d) % NDP, "slot": slot}, rank=-5)

    def weights(group, s, d):
        lse = stat_f[group, 0:1]
        delta = stat_f[group, 1:2]
        prob = jnp.exp(s - lse)
        dscore = (BETA * prob * (d - delta)).astype(BF)
        probs[group] = prob.astype(BF).reshape(2, SL, 128)
        dscores[group] = dscore.reshape(2, SL, 128)
        return dscore

    def own_weights():
        dscore = weights(dp, scores[...], dprobs[...])
        turned[...] = dscore.astype(F32).T.astype(BF)

    def query_part(h):
        def part(i, _):
            cut = pl.ds(pl.multiple_of(i * F, F), F)
            out = jnp.dot(turned[...], kv[0, :, :, cut].reshape(2 * SL, F), preferred_element_type=F32)
            rs[:, :, :, cut] = out.astype(BF).reshape(2, NX, 16, F)
            return 0
        lax.fori_loop(h * NF // 2, (h + 1) * NF // 2, part, 0)

    compute("own weights", ["merge x"], 0.4, own_weights, rank=0)
    for h in range(2):
        compute(f"query part {h}", ["own weights"], 0.6, lambda h=h: query_part(h), rank=0)
    low, high = slice(0, D // 2), slice(D // 2, D)
    for e, far, near in ((1, low, high), (-1, high, low)):
        link = "x+" if e > 0 else "x-"
        slot_in = 0 if e > 0 else 1
        transfer(f"ra {e}", [f"query part {0 if e > 0 else 1}"], link, 128 * KIB, lambda far=far: rs.at[:, (x + 2) % NX, :, far],
                 lambda s=slot_in: rs_a.at[s], lambda s=slot_in: rs_a.at[s], chip(e, 0, 0), rank=-2)
        transfer(f"rb {e} 0", [f"query part {1 if e > 0 else 0}"], link, 128 * KIB, lambda e=e, near=near: rs.at[:, (x + e + NX) % NX, :, near],
                 lambda s=slot_in, near=near: rs_x.at[s, :, :, near], lambda s=slot_in, near=near: rs_x.at[s, :, :, near],
                 chip(e, 0, 0), rank=-1)

        def add(e=e, far=far, slot_in=slot_in):
            to = (x + e + NX) % NX
            for i in range(NF // 2):
                cut = slice(far.start + i * F, far.start + (i + 1) * F)
                both = rs[:, to, :, cut].astype(F32) + rs_a[slot_in, :, :, i * F:(i + 1) * F].astype(F32)
                rs[:, to, :, cut] = both.astype(BF)

        compute(f"add {e}", [f"ra {e}"], 0.2, add, rank=0)
        transfer(f"rb {e} 1", [f"add {e}"], link, 128 * KIB, lambda e=e, far=far: rs.at[:, (x + e + NX) % NX, :, far],
                 lambda s=slot_in, far=far: rs_x.at[s, :, :, far], lambda s=slot_in, far=far: rs_x.at[s, :, :, far],
                 chip(e, 0, 0), rank=-1)

    def reduce_x():
        for i in range(NF):
            cut = slice(i * F, (i + 1) * F)
            total = rs[:, x, :, cut].astype(F32) + rs_x[0, :, :, cut].astype(F32) + rs_x[1, :, :, cut].astype(F32)
            rs_t[pl.ds(32 * i, 32), :] = total.reshape(32, F).astype(BF)
        laid = jnp.dot(gather_rows[...], rs_t[...], preferred_element_type=F32).astype(BF)
        rs_t[...] = laid

    compute("reduce x", [f"rb {e} {k}" for e in (1, -1) for k in range(2)], 0.6, reduce_x, rank=0)
    for d in range(1, NY):
        transfer(f"ry {d}", ["reduce x"], "y*" if d == 4 else "y+" if d < 4 else "y-", 32 * KIB,
                 lambda d=d: rs_t.at[pl.ds(pl.multiple_of(((y + d) % NY) * 32, 32), 32)],
                 lambda d=d: rs_y.at[d - 1], lambda d=d: rs_y.at[d - 1], chip(0, d, 0), hops=min(d, NY - d), rank=-3)

    def reduce_y():
        total = rs_t[pl.ds(pl.multiple_of(y * 32, 32), 32), :].astype(F32)
        for d in range(NY - 1):
            total += rs_y[d].astype(F32)
        rs_z[0:2] = total.astype(BF).reshape(2, 16, F)

    compute("reduce y", [f"ry {d}" for d in range(1, NY)], 0.3, reduce_y, rank=0)
    transfer("rz", ["reduce y"], "z*", 16 * KIB, lambda: rs_z.at[1 - zh], lambda: rs_z.at[2], lambda: rs_z.at[2],
             chip(0, 0, 4), hops=4, rank=-3)

    def finish_queries():
        total = rs_z[zh].astype(F32) + rs_z[2].astype(F32)
        lines = [jnp.concatenate([total[8 * r + i:8 * r + i + 1] for i in range(NF)], axis=1) for r in range(2)]
        qg_ref[...] = jnp.concatenate(lines, axis=0).astype(BF)

    compute("finish queries", ["rz"], 0.2, finish_queries, rank=12)

    def other_group(k):
        def run():
            group = (dp + k) % NDP
            s, d = products(group)
            weights(group, s, d)
        return run

    for k in range(1, NDP):
        zs = [k, k - 4]
        compute(f"group {k}", [f"rows {d} {a}" for d in zs for a in range(2)] + [f"sf {NDP - k}", "norm", "load 1", "kv 1"],
                1.6, other_group(k), rank=7)

    def gradients(core, j, store):
        left_k = jnp.concatenate([dscores[i, core] for i in range(NDP)], axis=1)
        left_v = jnp.concatenate([probs[i, core] for i in range(NDP)], axis=1)
        column = jnp.sum(left_k.astype(F32), axis=1, keepdims=True)
        for i in range(j * NF // PIECES, (j + 1) * NF // PIECES):
            cut = slice(i * F, (i + 1) * F)
            grad = jnp.dot(left_k, rows[0, :, :, :, cut].reshape(512, F), preferred_element_type=F32)
            store(i, 0, grad - column * kv[0, core, :, cut].astype(F32))
            store(i, 1, jnp.dot(left_v, rows[1, :, :, :, cut].reshape(512, F), preferred_element_type=F32))

    def store_out(i, n, value):
        cross_out[i, n] = value.astype(BF)

    def store_own(i, n, value):
        own[i, n] = value

    def storing(i, n):
        ref = vg_hbm if n else kg_hbm
        return pltpu.make_async_copy(outs.at[i, n], ref.at[:, i * F:(i + 1) * F], store_sem.at[i, n])

    def finish(j):
        for i in range(j * NF // PIECES, (j + 1) * NF // PIECES):
            for n in range(2):
                outs[i, n] = (own[i, n] + cross_in[i, n].astype(F32)).astype(BF)
                storing(i, n).start()

    groups = [f"group {k}" for k in range(1, NDP)] + ["own weights"]
    for j in range(PIECES):
        piece = pl.ds(j * NF // PIECES, NF // PIECES)
        compute(f"other {j}", groups, 0.7, lambda j=j: gradients(1 - c, j, store_out), rank=20)
        transfer(f"cx {j}", [f"other {j}"], "core", 2560 * KIB // PIECES, lambda p=piece: cross_out.at[p],
                 lambda p=piece: cross_in.at[p], lambda p=piece: cross_in.at[p], other_core, rank=0)
        compute(f"own {j}", groups, 0.7, lambda j=j: gradients(c, j, store_own), rank=21)
        compute(f"finish {j}", [f"own {j}", f"cx {j}"], 0.2, lambda j=j: finish(j), rank=22)

    assert len(index) <= TRANSFERS
    for what, name in plan.order():
        if what == "start":
            emit[name][0]().start()
        elif what == "wait":
            emit[name][1]().wait_recv()
        else:
            emit[name]()

    for name in index:
        emit[name][0]().wait_send()
    for i in range(NF):
        for n in range(2):
            storing(i, n).wait()


PIECES = 4
TRANSFERS = 224


def body(queries, keys, values, cotangent):
    vmem = pl.BlockSpec(memory_space=pltpu.VMEM)
    hbm = pl.BlockSpec(memory_space=pl.ANY)
    grads = pl.pallas_call(
        kernel,
        name="memory_backward",
        out_shape=(
            jax.ShapeDtypeStruct((2, D), BF),
            jax.ShapeDtypeStruct((SL, D), BF),
            jax.ShapeDtypeStruct((SL, D), BF),
        ),
        in_specs=[vmem, vmem, hbm, hbm],
        out_specs=(vmem, hbm, hbm),
        scratch_shapes=[
            pltpu.VMEM((NZ, 2, NX, NY, 16, F), BF),
            pltpu.VMEM((2, NDP, 2, 64, D), BF),
            pltpu.VMEM((2, 2, SL, D), BF),
            pltpu.VMEM((2 * SL, 128), F32),
            pltpu.VMEM((256, 256), BF),
            pltpu.VMEM((256, 256), BF),
            pltpu.VMEM((128, 2 * SL), BF),
            pltpu.VMEM((NDP, 2, SL, 128), BF),
            pltpu.VMEM((NDP, 2, SL, 128), BF),
            pltpu.VMEM((2 * SL, 128), F32),
            pltpu.VMEM((2 * SL, 128), F32),
            pltpu.VMEM((NY, 8, 128), F32),
            pltpu.VMEM((2 * NX, 8, 128), F32),
            pltpu.VMEM((NDP, 8, 128), F32),
            pltpu.VMEM((2, NX, 16, D), BF),
            pltpu.VMEM((2, 2, 16, D // 2), BF),
            pltpu.VMEM((2, 2, 16, D), BF),
            pltpu.VMEM((256, F), BF),
            pltpu.VMEM((NY - 1, 32, F), BF),
            pltpu.VMEM((3, 16, F), BF),
            pltpu.VMEM((NF, 2, SL, F), F32),
            pltpu.VMEM((NF, 2, SL, F), BF),
            pltpu.VMEM((NF, 2, SL, F), BF),
            pltpu.VMEM((NF, 2, SL, F), BF),
            pltpu.SemaphoreType.DMA((TRANSFERS,)),
            pltpu.SemaphoreType.DMA((TRANSFERS,)),
            pltpu.SemaphoreType.DMA((2,)),
            pltpu.SemaphoreType.DMA((NF, 2)),
        ],
        compiler_params=pltpu.CompilerParams(
            collective_id=0, has_side_effects=True, vmem_limit_bytes=56 * 2**20
        ),
    )(queries, cotangent, keys, values)
    return grads


def solution(mesh):
    rows = P(("dp", "slot"), None)
    slots = P("slot", None)
    return jax.shard_map(
        body,
        mesh=mesh,
        in_specs=(rows, slots, slots, rows),
        out_specs=(rows, slots, slots),
        check_vma=False,
    )
```

```python
import math

import jax
import jax.numpy as jnp
from jax import lax
from jax.experimental import pallas as pl
from jax.experimental.pallas import tpu as pltpu
from jax.sharding import PartitionSpec as P

MESH = pl.DeviceIdType.MESH
D = 4096
BETA = 1.25 * D ** (-0.5)
NX, NY, NZ, NDP = 4, 8, 8, 4
SL = 160
F = 512
NF = D // F
BF = jnp.bfloat16
F32 = jnp.float32


UNITS = ((0, 0), (0, 1), (4, 0), (4, 1), (3, 0), (3, 1), (-3, 0), (-3, 1), (2, 0), (-2, 1))

HOP_US = 2.3
FAR_US = 0.4
CORE_HOP_US = 1.5
LINK_RATE = 48e3
CORE_RATE = 500e3
BACKLOG_US = 1.0
FIRST_RANK = 0.5
START_US = 0.05
WAIT_US = 0.03


class Plan:
    def __init__(self):
        self.items = {}

        self.members = {}

    def transfer(self, name, needs, link, size, hops=1, rank=0, group=None):
        group = group or name
        self.members.setdefault(group, []).append(name)
        self.items[name] = dict(kind="t", needs=list(needs), link=link, size=size, hops=hops, rank=rank, group=group)

    def compute(self, name, needs, cost, rank=0):
        self.items[name] = dict(kind="c", needs=list(needs), cost=cost, rank=rank)

    def order(self):
        now = 0.0
        done, started, landing, arrivals, free, steps = set(), set(), {}, {}, {}, []
        group_of = {n: i.get("group", n) for n, i in self.items.items()}
        needs = {n: {group_of[d] for d in i["needs"]} for n, i in self.items.items()}
        left = set(group_of.values())
        while left:
            ready = [n for n in self.items if n not in started and needs[n] <= done]
            held = []
            sends = sorted((n for n in ready if self.items[n]["kind"] == "t"), key=lambda n: self.items[n]["rank"])
            for n in sends:
                i = self.items[n]
                rate, hop = (CORE_RATE, CORE_HOP_US) if i["link"] == "core" else (LINK_RATE, HOP_US)
                links = [i["link"][0] + w for w in "+-"] if i["link"].endswith("*") else [i["link"]]
                queued = max(free.get(link, 0.0) for link in links)
                if queued - now > BACKLOG_US and i["rank"] > 0:
                    held.append(queued - BACKLOG_US)
                    continue
                now += START_US
                for link in links:
                    free[link] = max(now, free.get(link, 0.0)) + i["size"] * i["hops"] / rate / len(links)
                landing[n] = max(free[link] for link in links) + hop + FAR_US * (i["hops"] - 1)
                started.add(n)
                steps.append(("start", n))
                group = i["group"]
                if all(m in started for m in self.members[group]):
                    arrivals[group] = max(landing[m] for m in self.members[group])
            first = min(arrivals, key=lambda n: (arrivals[n], n)) if arrivals else None
            if first is not None and arrivals[first] <= now:
                steps.append(("wait", first))
                arrivals.pop(first)
                done.add(first)
                left.discard(first)
                now += WAIT_US
                continue
            runs = sorted((n for n in ready if self.items[n]["kind"] == "c"), key=lambda n: self.items[n]["rank"])
            if runs:
                n = runs[0]
                now += self.items[n]["cost"]
                started.add(n)
                done.add(n)
                left.discard(n)
                steps.append(("run", n))
                continue
            if held and (first is None or min(held) < arrivals[first]):
                now = max(now, min(held)) + 0.001
                continue
            now = max(now, arrivals.pop(first)) + WAIT_US
            steps.append(("wait", first))
            done.add(first)
            left.discard(first)
        self.end = now
        return steps


def kernel(q_ref, g_ref, k_hbm, v_hbm, qg_ref, ownk_hbm, ownv_hbm, crossk_hbm, crossv_hbm,
           blocks, rows, kv, norm, spread, gather_rows, turned, probs, dscores, scores, dprobs,
           stat_y, stat_x, stat_f, rs, rs_a, rs_x, rs_t, rs_y, rs_z, own, cross,
           send_sem, recv_sem, load_sem, store_sem):
    dp = lax.axis_index("dp")
    slot = lax.axis_index("slot")
    c = slot % 2
    y = (slot // 2) % NY
    zh = (slot // 16) % 2
    x = slot // 32
    z = zh * NDP + dp

    def chip(dx, dy, dz):
        zz = (z + dz + NZ) % NZ
        return {"dp": zz % NDP, "slot": ((((x + dx + NX) % NX) * 2 + zz // NDP) * NY + (y + dy + NY) % NY) * 2 + c}

    other_core = {"dp": dp, "slot": slot + 1 - 2 * c}

    loads = []
    for n, src in enumerate((k_hbm, v_hbm)):
        cp = pltpu.make_async_copy(src, kv.at[n, c], load_sem.at[n])
        cp.start()
        loads.append(cp)

    barrier = pltpu.get_barrier_semaphore()
    peers = [chip(d, 0, 0) for d in range(1, NX)] + [chip(0, d, 0) for d in range(1, NY)]
    peers += [chip(0, 0, d) for d in range(1, NZ)] + [chip(d, 0, 4) for d in range(1, NX)] + [other_core]
    for p in peers:
        pl.semaphore_signal(barrier, inc=1, device_id=p, device_id_type=MESH)

    def to_rows16(ref):
        wide = ref[...].astype(F32)
        return jnp.concatenate([wide[r:r + 1, i * F:(i + 1) * F] for r in range(2) for i in range(NF)], axis=0).astype(BF)

    blocks[z, 0, x, y] = to_rows16(q_ref)
    blocks[z, 1, x, y] = to_rows16(g_ref)

    row = lax.broadcasted_iota(jnp.int32, (256, 256), 0)
    col = lax.broadcasted_iota(jnp.int32, (256, 256), 1)
    spread[...] = jnp.where(col == (row % 32) * NF + row // 32, 1.0, 0.0).astype(BF)
    want = (row % 8) * 32 + ((row // 16) % 2) * 16 + (row // 32) * 2 + (row // 8) % 2
    gather_rows[...] = jnp.where(col == want, 1.0, 0.0).astype(BF)

    pl.semaphore_wait(barrier, len(peers))

    plan = Plan()
    emit = {}
    send_index = {}
    recv_index = {}
    sent = {}

    def transfer(name, needs, link, size, src, dst, incoming, peer, hops=1, rank=0, group=None, whole=None, drain=None):
        plan.transfer(name, needs, link, size, hops, rank, group)
        r = recv_index.setdefault(group or name, len(recv_index))
        key, view = drain or (name, src)
        n = send_index.setdefault(key, len(send_index))
        if size:
            sent.setdefault(key, [view, n, peer, 0])[3] += size

        def out():
            return pltpu.make_async_remote_copy(
                src_ref=src(), dst_ref=dst(), send_sem=send_sem.at[n], recv_sem=recv_sem.at[r],
                device_id=peer, device_id_type=MESH)

        def into():
            ref = (whole or incoming)()
            return pltpu.make_async_remote_copy(
                src_ref=ref, dst_ref=ref, send_sem=send_sem.at[n], recv_sem=recv_sem.at[r],
                device_id=peer, device_id_type=MESH)

        emit[name] = (out, into)
        if group:
            emit[group] = (out, into)

    def compute(name, needs, cost, run, rank=0):
        plan.compute(name, needs, cost, rank)
        emit[name] = run

    def at(dz, a, dx, dy):
        xs = dx if not isinstance(dx, int) else (x + dx + NX) % NX
        ys = dy if not isinstance(dy, int) else (y + dy + NY) % NY
        return blocks.at[(z + dz + NZ) % NZ, a, xs, ys]

    def unit(dz, a):
        return blocks.at[(z + dz + NZ) % NZ, a]

    def move(name, needs, link, size, dz, a, dx, dy, step, hops=1, rank=0, **names):
        ex, ey, ez = step

        def shifted(d, e):
            return d if not isinstance(d, int) else d - e

        transfer(name, needs, link, size, lambda: at(dz, a, dx, dy), lambda: at(dz, a, dx, dy),
                 lambda: at(dz - ez, a, shifted(dx, ex), shifted(dy, ey)), chip(*step), hops, rank, **names)

    KIB = 1024
    every = slice(None)

    def of_unit(dz, a, part=None):
        if dz == 0 and a == 0:
            if part == "xp":
                return "own xp", lambda: blocks.at[0, 0, 0, pl.ds(0, 3)]
            return "own yl", lambda: blocks.at[0, 0, :, pl.ds(0, 7)]
        return f"unit {dz} {a}", lambda: unit(dz, a)

    for ez, a in ((4, 0), (4, 1), (-3, 0), (3, 0), (-3, 1), (3, 1), (-2, 0), (2, 1)):
        move(f"z1 {ez} {a}", [], "z*" if ez == 4 else "z+" if ez > 0 else "z-", 16 * KIB, 0, a, 0, 0, (0, 0, ez),
             hops=abs(ez), rank=0 if ez == 4 else FIRST_RANK, drain=of_unit(4 if ez == 4 else -ez, a))

    def first_hop(dz, a):
        return [] if dz == 0 else [f"z1 4 {a}" if dz == 4 else f"z1 {-dz} {a}"]

    def line_parts(dz):
        return (0, 1) if dz in (0, 4) else (None,)

    arrived = {(dz, a): [] for dz in range(-3, 5) for a in range(2)}
    for u, (dz, a) in enumerate(UNITS):
        have = first_hop(dz, a)
        near = dz in (0, 4)
        rank = 0 if near else u
        firsts = []
        if a == 0:
            for e in (1, -1, 2):
                name = f"xp {dz} {e}"
                move(name, have, "x*" if e == 2 else "x-" if e < 0 else "x+", 16 * KIB, dz, 0, 0, 0, (e, 0, 0), hops=abs(e), rank=min(rank, FIRST_RANK),
                     group=f"xp {dz}", whole=lambda: blocks.at[0, 0, 0, pl.ds(0, 3)], drain=of_unit(dz, a, "xp"))
                firsts.append(name)
            for k in range(4):
                for way in (1, -1):
                    for h in line_parts(dz):
                        if k == 3 and h == (1 if way > 0 else 0):
                            continue
                        needs = firsts + have if k == 0 else [f"yl {dz} {way} {k - 1} {h}"]
                        half = (pl.ds(0, 2) if way > 0 else pl.ds(2, 2)) if k == 3 else every if h is None else pl.ds(2 * h, 2)
                        name = f"yl {dz} {way} {k} {h}"
                        move(name, needs, "y+" if way > 0 else "y-", (64 if k < 3 and h is None else 32) * KIB,
                             dz, 0, half, -way * k, (0, way, 0), rank=rank, drain=of_unit(dz, a))
                        arrived[dz, 0].append(name)
        else:
            if near:
                for d in range(1, NY):
                    name = f"yp {dz} {d}"
                    move(name, have, "y*" if d == 4 else "y+" if d < 4 else "y-", 16 * KIB, dz, 1, 0, 0, (0, d, 0), hops=min(d, NY - d), rank=min(rank, FIRST_RANK),
                         group=f"yp {dz}", whole=lambda: blocks.at[0, 0, 0, pl.ds(0, 7)], drain=of_unit(dz, a))
                    firsts.append(name)
            else:
                for way in (1, -1):
                    for k in range(4 if (way > 0) == (u % 4 == 1) else 3):
                        name = f"yp {dz} {way} {k}"
                        needs = have if k == 0 else [f"yp {dz} {way} {k - 1}"]
                        move(name, needs, "y+" if way > 0 else "y-", 16 * KIB, dz, 1, 0, -way * k, (0, way, 0), rank=min(rank, FIRST_RANK),
                             drain=of_unit(dz, a))
                        firsts.append(name)
            for e in (1, -1):
                for k in range(2):
                    needs = firsts + have if k == 0 else [f"xl {dz} {e} 0"]
                    name = f"xl {dz} {e} {k}"
                    half = every if k == 0 else (pl.ds(0, 4) if e > 0 else pl.ds(4, 4))
                    move(name, needs, "x+" if e > 0 else "x-", (128 if k == 0 else 64) * KIB, dz, 1, -e * k, half,
                         (e, 0, 0), rank=rank, drain=of_unit(dz, a))
                    arrived[dz, 1].append(name)
        arrived[dz, a] += firsts + have
        if dz == 0:
            own_line = (firsts if a == 0 else own_line[0], firsts)

    for ez in (1, -1):
        link = "z+" if ez > 0 else "z-"
        lines = [(0, "own", own_line[0], 64, every, 0), (1, "own", own_line[1], 128, 0, every)]
        for way in (1, -1):
            for k in range(4):
                half = every if k < 3 else (pl.ds(0, 2) if way > 0 else pl.ds(2, 2))
                needs = [n for n in arrived[0, 0] if n.startswith(f"yl 0 {way} {k}")]
                lines.append((0, f"{way} {k}", needs, 64 if k < 3 else 32, half, -way * (k + 1)))
            for k in range(2):
                half = every if k < 1 else (pl.ds(0, 4) if way > 0 else pl.ds(4, 4))
                lines.append((1, f"{way} {k}", [f"xl 0 {way} {k}"], 128 if k < 1 else 64, -way * (k + 1), half))
        for a, label, needs, size, dx, dy in lines:
            name = f"zl {a} {ez} {label}"
            passes = a == (0 if ez > 0 else 1)
            as_one = {} if passes else dict(group=f"zl {a} {ez}", whole=lambda ez=ez, a=a: unit(-ez, a))
            move(name, needs, link, size * KIB, 0, a, dx, dy, (0, 0, ez), rank=3,
                 drain=(f"zl {ez}", lambda: blocks.at[0]), **as_one)
            arrived[-ez, a].append(name)
            if passes:
                further = f"zf {a} {ez} {label}"
                move(further, [name], link, size * KIB, -ez, a, dx, dy, (0, 0, ez), rank=4, group=f"zf {ez}",
                     whole=lambda ez=ez, a=a: unit(-2 * ez, a), drain=("zf", lambda: blocks.at[0]))
                arrived[-2 * ez, a].append(further)

    def load(n):
        return lambda: loads[n].wait()

    for n in range(2):
        compute(f"load {n}", [], 0.6, load(n), rank=5)
        transfer(f"kv {n}", [f"load {n}"], "core", 1280 * KIB, lambda n=n: kv.at[n, c], lambda n=n: kv.at[n, c],
                 lambda n=n: kv.at[n, 1 - c], other_core, rank=9, drain=("kv", lambda: kv.at[:, c]))

    def key_norm():
        for half in range(2):
            def add(i, total):
                part = kv[0, half, :, pl.ds(pl.multiple_of(i * 128, 128), 128)].astype(F32)
                return total + part * part
            total = lax.fori_loop(0, D // 128, add, jnp.zeros((SL, 128), F32))
            norm[pl.ds(half * SL, SL), :] = jnp.broadcast_to(
                (0.5 * BETA) * jnp.sum(total, axis=1, keepdims=True), (SL, 128))

    compute("norm", ["load 0", "kv 0"], 1.1, key_norm, rank=6)

    def relayout(dz, a):
        def run():
            zz = (z + dz + NZ) % NZ
            for h in range(2):
                got = blocks[zz, a, 2 * h:2 * h + 2].reshape(256, F)
                laid = jnp.dot(spread[...], got, preferred_element_type=F32).astype(BF)
                for i in range(NF):
                    rows[a, zz % NDP, zz // NDP, pl.ds(32 * h, 32), i * F:(i + 1) * F] = laid[i * 32:(i + 1) * 32]
        return run

    for dz in range(-3, 5):
        for a in range(2):
            compute(f"rows {dz} {a}", arrived[dz, a], 0.12, relayout(dz, a), rank=3 if dz in (0, 4) else 8)

    def products(group):
        def one(n):
            return lax.dot_general(kv[n].reshape(2 * SL, D), rows[n, group].reshape(128, D), (((1,), (1,)), ((), ())),
                                   preferred_element_type=F32)
        return BETA * one(0) - norm[...], one(1)

    def own_scores():
        s, d = products(dp)
        scores[...] = s
        dprobs[...] = d
        top = jnp.max(s, axis=0, keepdims=True)
        e = jnp.exp(s - top)
        stat_y[y, 0:1] = top
        stat_y[y, 1:2] = jnp.sum(e, axis=0, keepdims=True)
        stat_y[y, 2:3] = jnp.sum(e * d, axis=0, keepdims=True)
        stat_y[y, 3:8] = jnp.zeros((5, 128), F32)

    def merge(ref):
        parts = [ref[i] for i in range(8)]
        top = parts[0][0:1]
        for p in parts[1:]:
            top = jnp.maximum(top, p[0:1])
        total = jnp.zeros((1, 128), F32)
        weighted = jnp.zeros((1, 128), F32)
        for p in parts:
            scale = jnp.exp(p[0:1] - top)
            total += p[1:2] * scale
            weighted += p[2:3] * scale
        return top, total, weighted

    compute("own scores", ["rows 0 0", "rows 0 1", "rows 4 0", "rows 4 1", "norm", "load 1", "kv 1"], 1.3, own_scores, rank=1)
    stats = ("stats", lambda: norm.at[pl.ds(0, 17 * 8)])
    for d in range(1, NY):
        transfer(f"sy {d}", ["own scores"], f"sy{d}", 4 * KIB, lambda: stat_y.at[y], lambda: stat_y.at[y],
                 lambda: stat_y.at[0], chip(0, d, 0), rank=-5,
                 group="sy", whole=lambda: stat_y.at[pl.ds(0, 7)], drain=stats)

    place = x * 2 + zh

    def merge_y():
        top, total, weighted = merge(stat_y)
        stat_x[place, 0:1] = top
        stat_x[place, 1:2] = total
        stat_x[place, 2:3] = weighted
        stat_x[place, 3:8] = jnp.zeros((5, 128), F32)

    compute("merge y", [f"sy {d}" for d in range(1, NY)], 0.3, merge_y, rank=0)
    for d in range(NX):
        for e in range(2):
            if d or e:
                transfer(f"sx {d} {e}", ["merge y"], f"sx{d}{e}", 4 * KIB, lambda: stat_x.at[place], lambda: stat_x.at[place],
                         lambda: stat_x.at[0], chip(d, 0, 4 * e), rank=-5,
                         group="sx", whole=lambda: stat_x.at[pl.ds(0, 7)], drain=stats)

    def merge_x():
        top, total, weighted = merge(stat_x)
        stat_f[dp, 0:1] = top + jnp.log(total)
        stat_f[dp, 1:2] = weighted / total
        stat_f[dp, 2:8] = jnp.zeros((6, 128), F32)

    compute("merge x", [f"sx {d} {e}" for d in range(NX) for e in range(2) if d or e], 0.3, merge_x, rank=0)
    for d in range(1, NDP):
        transfer(f"sf {d}", ["merge x"], f"sf{d}", 4 * KIB, lambda: stat_f.at[dp], lambda: stat_f.at[dp],
                 lambda: stat_f.at[0], {"dp": (dp + d) % NDP, "slot": slot}, rank=-5,
                 group="sf", whole=lambda: stat_f.at[pl.ds(0, 3)], drain=stats)

    def weights(group, s, d):
        lse = stat_f[group, 0:1]
        delta = stat_f[group, 1:2]
        prob = jnp.exp(s - lse)
        dscore = (BETA * prob * (d - delta)).astype(BF)
        probs[group] = prob.astype(BF).reshape(2, SL, 128)
        dscores[group] = dscore.reshape(2, SL, 128)
        return dscore

    def own_weights():
        dscore = weights(dp, scores[...], dprobs[...])
        turned[...] = dscore.astype(F32).T.astype(BF)

    def query_part(h):
        def part(i, _):
            cut = pl.ds(pl.multiple_of(i * F, F), F)
            out = jnp.dot(turned[...], kv[0, :, :, cut].reshape(2 * SL, F), preferred_element_type=F32)
            rs[:, :, :, cut] = out.astype(BF).reshape(2, NX, 16, F)
            return 0
        lax.fori_loop(h * NF // 2, (h + 1) * NF // 2, part, 0)

    compute("own weights", ["merge x"], 0.4, own_weights, rank=0)
    for h in range(2):
        compute(f"query part {h}", ["own weights"], 0.6, lambda h=h: query_part(h), rank=0)
    parts = ("parts", lambda: rs.at[:, pl.ds(0, 3)])
    low, high = slice(0, D // 2), slice(D // 2, D)
    for e, far, near in ((1, low, high), (-1, high, low)):
        link = "x+" if e > 0 else "x-"
        slot_in = 0 if e > 0 else 1
        transfer(f"ra {e}", [f"query part {0 if e > 0 else 1}"], link, 128 * KIB, lambda far=far: rs.at[:, (x + 2) % NX, :, far],
                 lambda s=slot_in: rs_a.at[s], lambda s=slot_in: rs_a.at[s], chip(e, 0, 0), rank=-2, drain=parts)
        transfer(f"rb {e} 0", [f"query part {1 if e > 0 else 0}"], link, 128 * KIB, lambda e=e, near=near: rs.at[:, (x + e + NX) % NX, :, near],
                 lambda s=slot_in, near=near: rs_x.at[s, :, :, near], lambda s=slot_in, near=near: rs_x.at[s, :, :, near],
                 chip(e, 0, 0), rank=-1, drain=parts)

        def add(e=e, far=far, slot_in=slot_in):
            to = (x + e + NX) % NX
            for i in range(NF // 2):
                cut = slice(far.start + i * F, far.start + (i + 1) * F)
                both = rs[:, to, :, cut].astype(F32) + rs_a[slot_in, :, :, i * F:(i + 1) * F].astype(F32)
                rs[:, to, :, cut] = both.astype(BF)

        compute(f"add {e}", [f"ra {e}"], 0.2, add, rank=0)
        transfer(f"rb {e} 1", [f"add {e}"], link, 128 * KIB, lambda e=e, far=far: rs.at[:, (x + e + NX) % NX, :, far],
                 lambda s=slot_in, far=far: rs_x.at[s, :, :, far], lambda s=slot_in, far=far: rs_x.at[s, :, :, far],
                 chip(e, 0, 0), rank=-1, drain=parts)

    def reduce_x():
        for i in range(NF):
            cut = slice(i * F, (i + 1) * F)
            total = rs[:, x, :, cut].astype(F32) + rs_x[0, :, :, cut].astype(F32) + rs_x[1, :, :, cut].astype(F32)
            rs_t[pl.ds(32 * i, 32), :] = total.reshape(32, F).astype(BF)
        laid = jnp.dot(gather_rows[...], rs_t[...], preferred_element_type=F32).astype(BF)
        rs_t[...] = laid

    compute("reduce x", [f"rb {e} {k}" for e in (1, -1) for k in range(2)], 0.6, reduce_x, rank=0)
    for d in range(1, NY):
        transfer(f"ry {d}", ["reduce x"], "y*" if d == 4 else "y+" if d < 4 else "y-", 32 * KIB,
                 lambda d=d: rs_t.at[pl.ds(pl.multiple_of(((y + d) % NY) * 32, 32), 32)],
                 lambda d=d: rs_y.at[d - 1], lambda d=d: rs_y.at[d - 1], chip(0, d, 0), hops=min(d, NY - d), rank=-3,
                 group="ry", whole=lambda: rs_y, drain=("ry", lambda: rs_y))

    def reduce_y():
        total = rs_t[pl.ds(pl.multiple_of(y * 32, 32), 32), :].astype(F32)
        for d in range(NY - 1):
            total += rs_y[d].astype(F32)
        rs_z[0:2] = total.astype(BF).reshape(2, 16, F)

    compute("reduce y", [f"ry {d}" for d in range(1, NY)], 0.3, reduce_y, rank=0)
    transfer("rz", ["reduce y"], "z*", 16 * KIB, lambda: rs_z.at[1 - zh], lambda: rs_z.at[2], lambda: rs_z.at[2],
             chip(0, 0, 4), hops=4, rank=-3, drain=of_unit(0, 1))

    def finish_queries():
        total = rs_z[zh].astype(F32) + rs_z[2].astype(F32)
        lines = [jnp.concatenate([total[8 * r + i:8 * r + i + 1] for i in range(NF)], axis=1) for r in range(2)]
        qg_ref[...] = jnp.concatenate(lines, axis=0)

    compute("finish queries", ["rz"], 0.2, finish_queries, rank=12)

    def other_group(k):
        def run():
            group = (dp + k) % NDP
            s, d = products(group)
            weights(group, s, d)
        return run

    for k in range(1, NDP):
        zs = [k, k - 4]
        compute(f"group {k}", [f"rows {d} {a}" for d in zs for a in range(2)] + [f"sf {NDP - k}", "norm", "load 1", "kv 1"],
                1.3, other_group(k), rank=7)

    def gradients(core, j, store):
        left_k = jnp.concatenate([dscores[i, core] for i in range(NDP)], axis=1)
        left_v = jnp.concatenate([probs[i, core] for i in range(NDP)], axis=1)
        column = jnp.sum(left_k.astype(F32), axis=1, keepdims=True)
        for i in range(j * NF // PIECES, (j + 1) * NF // PIECES):
            cut = slice(i * F, (i + 1) * F)
            grad = jnp.dot(left_k, rows[0, :, :, :, cut].reshape(512, F), preferred_element_type=F32)
            store(i, 0, grad - column * kv[0, core, :, cut].astype(F32))
            store(i, 1, jnp.dot(left_v, rows[1, :, :, :, cut].reshape(512, F), preferred_element_type=F32))

    groups = [f"group {k}" for k in range(1, NDP)] + ["own weights"]
    wide = D // PIECES

    def store_in(ref):
        def store(i, n, value):
            ref[n, :, i * F:(i + 1) * F] = value.astype(BF)
        return store

    def storing(j, n):
        cut = pl.ds(j * wide, wide)
        return pltpu.make_async_copy(own.at[n, :, cut], (ownv_hbm if n else ownk_hbm).at[:, cut], store_sem)

    def own_part(j):
        gradients(c, j, store_in(own))
        for n in range(2):
            storing(j, n).start()

    for j in range(PIECES):
        cut = pl.ds(j * wide, wide)
        compute(f"other {j}", groups, 0.3, lambda j=j: gradients(1 - c, j, store_in(cross)), rank=20)
        for n, ref in enumerate((crossk_hbm, crossv_hbm)):
            transfer(f"cx {j} {n}", [f"other {j}"], "core", SL * wide * 2, lambda n=n, cut=cut: cross.at[n, :, cut],
                     lambda ref=ref, cut=cut: ref.at[:, cut], lambda ref=ref: ref, other_core, rank=0,
                     group=f"cx {n}", whole=lambda ref=ref: ref, drain=("cx", lambda: cross))
        compute(f"own {j}", groups, 0.3, lambda j=j: own_part(j), rank=21)

    assert len(recv_index) <= RECEIVES and len(send_index) <= SENDS
    for what, name in plan.order():
        if what == "start":
            emit[name][0]().start()
        elif what == "wait":
            emit[name][1]().wait_recv()
        else:
            emit[name]()

    for view, n, peer, size in sent.values():
        ref = view()
        assert math.prod(ref.shape) * jnp.dtype(ref.dtype).itemsize == size
        pltpu.make_async_remote_copy(
            src_ref=ref, dst_ref=ref, send_sem=send_sem.at[n], recv_sem=recv_sem.at[0],
            device_id=peer, device_id_type=MESH).wait_send()
    pltpu.make_async_copy(own, own, store_sem).wait()


PIECES = 4
SENDS = 19
RECEIVES = 150


def body(queries, keys, values, cotangent):
    vmem = pl.BlockSpec(memory_space=pltpu.VMEM)
    hbm = pl.BlockSpec(memory_space=pl.ANY)
    query, own_k, own_v, cross_k, cross_v = pl.pallas_call(
        kernel,
        name="memory_backward",
        out_shape=(
            jax.ShapeDtypeStruct((2, D), F32),
            *[jax.ShapeDtypeStruct((SL, D), BF)] * 4,
        ),
        in_specs=[vmem, vmem, hbm, hbm],
        out_specs=(vmem, hbm, hbm, hbm, hbm),
        scratch_shapes=[
            pltpu.VMEM((NZ, 2, NX, NY, 16, F), BF),
            pltpu.VMEM((2, NDP, 2, 64, D), BF),
            pltpu.VMEM((2, 2, SL, D), BF),
            pltpu.VMEM((2 * SL, 128), F32),
            pltpu.VMEM((256, 256), BF),
            pltpu.VMEM((256, 256), BF),
            pltpu.VMEM((128, 2 * SL), BF),
            pltpu.VMEM((NDP, 2, SL, 128), BF),
            pltpu.VMEM((NDP, 2, SL, 128), BF),
            pltpu.VMEM((2 * SL, 128), F32),
            pltpu.VMEM((2 * SL, 128), F32),
            pltpu.VMEM((NY, 8, 128), F32),
            pltpu.VMEM((2 * NX, 8, 128), F32),
            pltpu.VMEM((NDP, 8, 128), F32),
            pltpu.VMEM((2, NX, 16, D), BF),
            pltpu.VMEM((2, 2, 16, D // 2), BF),
            pltpu.VMEM((2, 2, 16, D), BF),
            pltpu.VMEM((256, F), BF),
            pltpu.VMEM((NY - 1, 32, F), BF),
            pltpu.VMEM((3, 16, F), BF),
            pltpu.VMEM((2, SL, D), BF),
            pltpu.VMEM((2, SL, D), BF),
            pltpu.SemaphoreType.DMA((SENDS,)),
            pltpu.SemaphoreType.DMA((RECEIVES,)),
            pltpu.SemaphoreType.DMA((2,)),
            pltpu.SemaphoreType.DMA,
        ],
        compiler_params=pltpu.CompilerParams(
            collective_id=0, has_side_effects=True, vmem_limit_bytes=56 * 2**20
        ),
    )(queries, cotangent, keys, values)
    key = (own_k.astype(F32) + cross_k.astype(F32)).astype(BF)
    value = (own_v.astype(F32) + cross_v.astype(F32)).astype(BF)
    return query.astype(BF), key, value


def solution(mesh):
    rows = P(("dp", "slot"), None)
    slots = P("slot", None)
    return jax.shard_map(
        body,
        mesh=mesh,
        in_specs=(rows, slots, slots, rows),
        out_specs=(rows, slots, slots),
        check_vma=False,
    )
```

```python
import math

import jax
import jax.numpy as jnp
from jax import lax
from jax.experimental import pallas as pl
from jax.experimental.pallas import tpu as pltpu
from jax.sharding import PartitionSpec as P

MESH = pl.DeviceIdType.MESH
D = 4096
BETA = 1.25 * D ** (-0.5)
NX, NY, NZ, NDP = 4, 8, 8, 4
SL = 160
F = 512
NF = D // F
BF = jnp.bfloat16
F32 = jnp.float32


UNITS = ((0, 0, "xy"), (0, 1, "yx"), (4, 0, "xy"), (4, 1, "yx"), (3, 0, "xy"), (3, 1, "yx"), (-3, 0, "xy"), (-3, 1, "yx"),
         (2, 0, "xy"), (-2, 1, "yx"))
RANKS = {
    "first -2 1": 0.5, "first -3 0": 9, "first -3 1": 5, "first 0 0": 5, "first 0 1": 9,
    "first 2 0": 8, "first 3 0": 9, "first 3 1": 3, "first 4 0": 2, "first 4 1": 0,
    "line -2 1": 8, "line -3 0": 5, "line -3 1": 0, "line 0 0": 3, "line 0 1": 2,
    "line 2 0": 7, "line 3 0": 8, "line 3 1": 9, "line 4 0": 0, "line 4 1": 7,
    "z1 -2 0": 5, "z1 -3 0": 9, "z1 -3 1": 8, "z1 2 1": 8, "z1 3 0": 7,
    "z1 3 1": 9, "z1 4 0": 3, "z1 4 1": 4, "zf -1": 3, "zf 1": 2,
    "zl 0 -1": 8, "zl 0 1": 3, "zl 1 -1": 9, "zl 1 1": 0,
}

HOP_US = 2.3
FAR_US = 0.4
CORE_HOP_US = 1.5
LINK_RATE = 48e3
CORE_RATE = 500e3
BACKLOG_US = 0.1
START_US = 0.05
WAIT_US = 0.03


class Plan:
    def __init__(self):
        self.items = {}

        self.members = {}

    def transfer(self, name, needs, link, size, hops=1, rank=0, group=None):
        group = group or name
        self.members.setdefault(group, []).append(name)
        self.items[name] = dict(kind="t", needs=list(needs), link=link, size=size, hops=hops, rank=rank, group=group)

    def compute(self, name, needs, cost, rank=0):
        self.items[name] = dict(kind="c", needs=list(needs), cost=cost, rank=rank)

    def order(self):
        now = 0.0
        done, started, landing, arrivals, free, steps = set(), set(), {}, {}, {}, []
        group_of = {n: i.get("group", n) for n, i in self.items.items()}
        needs = {n: {group_of[d] for d in i["needs"]} for n, i in self.items.items()}
        left = set(group_of.values())
        while left:
            ready = [n for n in self.items if n not in started and needs[n] <= done]
            held = []
            sends = sorted((n for n in ready if self.items[n]["kind"] == "t"), key=lambda n: self.items[n]["rank"])
            for n in sends:
                i = self.items[n]
                rate, hop = (CORE_RATE, CORE_HOP_US) if i["link"] == "core" else (LINK_RATE, HOP_US)
                links = [i["link"][0] + w for w in "+-"] if i["link"].endswith("*") else [i["link"]]
                queued = max(free.get(link, 0.0) for link in links)
                if queued - now > BACKLOG_US and i["rank"] > 0:
                    held.append(queued - BACKLOG_US)
                    continue
                now += START_US
                for link in links:
                    free[link] = max(now, free.get(link, 0.0)) + i["size"] * i["hops"] / rate / len(links)
                landing[n] = max(free[link] for link in links) + hop + FAR_US * (i["hops"] - 1)
                started.add(n)
                steps.append(("start", n))
                group = i["group"]
                if all(m in started for m in self.members[group]):
                    arrivals[group] = max(landing[m] for m in self.members[group])
            first = min(arrivals, key=lambda n: (arrivals[n], n)) if arrivals else None
            if first is not None and arrivals[first] <= now:
                steps.append(("wait", first))
                arrivals.pop(first)
                done.add(first)
                left.discard(first)
                now += WAIT_US
                continue
            runs = sorted((n for n in ready if self.items[n]["kind"] == "c"), key=lambda n: self.items[n]["rank"])
            if runs:
                n = runs[0]
                now += self.items[n]["cost"]
                started.add(n)
                done.add(n)
                left.discard(n)
                steps.append(("run", n))
                continue
            if held and (first is None or min(held) < arrivals[first]):
                now = max(now, min(held)) + 0.001
                continue
            now = max(now, arrivals.pop(first)) + WAIT_US
            steps.append(("wait", first))
            done.add(first)
            left.discard(first)
        self.end = now
        return steps


def kernel(q_ref, g_ref, k_hbm, v_hbm, qg_ref, ownk_hbm, ownv_hbm, crossk_hbm, crossv_hbm,
           blocks, rows, kv, norm, spread, gather_rows, turned, probs, dscores, scores, dprobs,
           stat_y, stat_x, stat_f, rs, rs_a, rs_x, rs_t, rs_y, rs_z, own, cross,
           send_sem, recv_sem, load_sem, store_sem):
    dp = lax.axis_index("dp")
    slot = lax.axis_index("slot")
    c = slot % 2
    y = (slot // 2) % NY
    zh = (slot // 16) % 2
    x = slot // 32
    z = zh * NDP + dp

    def chip(dx, dy, dz):
        zz = (z + dz + NZ) % NZ
        return {"dp": zz % NDP, "slot": ((((x + dx + NX) % NX) * 2 + zz // NDP) * NY + (y + dy + NY) % NY) * 2 + c}

    other_core = {"dp": dp, "slot": slot + 1 - 2 * c}

    loads = []
    for n, src in enumerate((k_hbm, v_hbm)):
        cp = pltpu.make_async_copy(src, kv.at[n, c], load_sem.at[n])
        cp.start()
        loads.append(cp)

    barrier = pltpu.get_barrier_semaphore()
    peers = [chip(d, 0, 0) for d in range(1, NX)] + [chip(0, d, 0) for d in range(1, NY)]
    peers += [chip(0, 0, d) for d in range(1, NZ)] + [chip(d, 0, 4) for d in range(1, NX)] + [other_core]
    for p in peers:
        pl.semaphore_signal(barrier, inc=1, device_id=p, device_id_type=MESH)

    def to_rows16(ref):
        wide = ref[...].astype(F32)
        return jnp.concatenate([wide[r:r + 1, i * F:(i + 1) * F] for r in range(2) for i in range(NF)], axis=0).astype(BF)

    blocks[z, 0, x, y] = to_rows16(q_ref)
    blocks[z, 1, x, y] = to_rows16(g_ref)

    row = lax.broadcasted_iota(jnp.int32, (256, 256), 0)
    col = lax.broadcasted_iota(jnp.int32, (256, 256), 1)
    spread[...] = jnp.where(col == (row % 32) * NF + row // 32, 1.0, 0.0).astype(BF)
    want = (row % 8) * 32 + ((row // 16) % 2) * 16 + (row // 32) * 2 + (row // 8) % 2
    gather_rows[...] = jnp.where(col == want, 1.0, 0.0).astype(BF)

    pl.semaphore_wait(barrier, len(peers))

    plan = Plan()
    emit = {}
    send_index = {}
    recv_index = {}
    sent = {}

    def transfer(name, needs, link, size, src, dst, incoming, peer, hops=1, rank=0, group=None, whole=None, drain=None):
        plan.transfer(name, needs, link, size, hops, rank, group)
        r = recv_index.setdefault(group or name, len(recv_index))
        key, view = drain or (name, src)
        n = send_index.setdefault(key, len(send_index))
        if size:
            sent.setdefault(key, [view, n, peer, 0])[3] += size

        def out():
            return pltpu.make_async_remote_copy(
                src_ref=src(), dst_ref=dst(), send_sem=send_sem.at[n], recv_sem=recv_sem.at[r],
                device_id=peer, device_id_type=MESH)

        def into():
            ref = (whole or incoming)()
            return pltpu.make_async_remote_copy(
                src_ref=ref, dst_ref=ref, send_sem=send_sem.at[n], recv_sem=recv_sem.at[r],
                device_id=peer, device_id_type=MESH)

        emit[name] = (out, into)
        if group:
            emit[group] = (out, into)

    def compute(name, needs, cost, run, rank=0):
        plan.compute(name, needs, cost, rank)
        emit[name] = run

    def at(dz, a, dx, dy):
        xs = dx if not isinstance(dx, int) else (x + dx + NX) % NX
        ys = dy if not isinstance(dy, int) else (y + dy + NY) % NY
        return blocks.at[(z + dz + NZ) % NZ, a, xs, ys]

    def unit(dz, a):
        return blocks.at[(z + dz + NZ) % NZ, a]

    def move(name, needs, link, size, dz, a, dx, dy, step, hops=1, rank=0, **names):
        ex, ey, ez = step

        def shifted(d, e):
            return d if not isinstance(d, int) else d - e

        transfer(name, needs, link, size, lambda: at(dz, a, dx, dy), lambda: at(dz, a, dx, dy),
                 lambda: at(dz - ez, a, shifted(dx, ex), shifted(dy, ey)), chip(*step), hops, rank, **names)

    KIB = 1024
    every = slice(None)

    def of_unit(dz, a, part=None):
        if dz == 0 and a == 0:
            if part == "xp":
                return "own xp", lambda: blocks.at[0, 0, 0, pl.ds(0, 3)]
            return "own yl", lambda: blocks.at[0, 0, :, pl.ds(0, 7)]
        return f"unit {dz} {a}", lambda: unit(dz, a)

    for ez, a in ((4, 0), (4, 1), (-3, 0), (3, 0), (-3, 1), (3, 1), (-2, 0), (2, 1)):
        move(f"z1 {ez} {a}", [], "z*" if ez == 4 else "z+" if ez > 0 else "z-", 16 * KIB, 0, a, 0, 0, (0, 0, ez),
             hops=abs(ez), rank=RANKS.get(f"z1 {ez} {a}", 1), drain=of_unit(4 if ez == 4 else -ez, a))

    def first_hop(dz, a):
        return [] if dz == 0 else [f"z1 4 {a}" if dz == 4 else f"z1 {-dz} {a}"]

    def line_parts(dz):
        return (0, 1) if dz in (0, 4) else (None,)

    arrived = {(dz, a): [] for dz in range(-3, 5) for a in range(2)}
    for u, (dz, a, route) in enumerate(UNITS):
        have = first_hop(dz, a)
        near = dz in (0, 4)
        first, rank = RANKS.get(f"first {dz} {a}", 1), RANKS.get(f"line {dz} {a}", 2)
        firsts = []
        if route == "xy":
            for e in (1, -1, 2):
                name = f"xp {dz} {a} {e}"
                move(name, have, "x*" if e == 2 else "x-" if e < 0 else "x+", 16 * KIB, dz, a, 0, 0, (e, 0, 0), hops=abs(e), rank=first,
                     group=f"xp {dz} {a}", whole=lambda: blocks.at[0, 0, 0, pl.ds(0, 3)], drain=of_unit(dz, a, "xp"))
                firsts.append(name)
            for k in range(4):
                for way in (1, -1):
                    for h in line_parts(dz):
                        if k == 3 and h == (1 if way > 0 else 0):
                            continue
                        needs = firsts + have if k == 0 else [f"yl {dz} {a} {way} {k - 1} {h}"]
                        half = (pl.ds(0, 2) if way > 0 else pl.ds(2, 2)) if k == 3 else every if h is None else pl.ds(2 * h, 2)
                        name = f"yl {dz} {a} {way} {k} {h}"
                        move(name, needs, "y+" if way > 0 else "y-", (64 if k < 3 and h is None else 32) * KIB,
                             dz, a, half, -way * k, (0, way, 0), rank=rank, drain=of_unit(dz, a))
                        arrived[dz, a].append(name)
        else:
            if near:
                for d in range(1, NY):
                    name = f"yp {dz} {a} {d}"
                    move(name, have, "y*" if d == 4 else "y+" if d < 4 else "y-", 16 * KIB, dz, a, 0, 0, (0, d, 0), hops=min(d, NY - d), rank=first,
                         group=f"yp {dz} {a}", whole=lambda: blocks.at[0, 0, 0, pl.ds(0, 7)], drain=of_unit(dz, a))
                    firsts.append(name)
            else:
                for way in (1, -1):
                    for k in range(4 if (way > 0) == (u % 4 == 1) else 3):
                        name = f"yp {dz} {a} {way} {k}"
                        needs = have if k == 0 else [f"yp {dz} {a} {way} {k - 1}"]
                        move(name, needs, "y+" if way > 0 else "y-", 16 * KIB, dz, a, 0, -way * k, (0, way, 0), rank=first,
                             drain=of_unit(dz, a))
                        firsts.append(name)
            for e in (1, -1):
                for k in range(2):
                    needs = firsts + have if k == 0 else [f"xl {dz} {a} {e} 0"]
                    name = f"xl {dz} {a} {e} {k}"
                    half = every if k == 0 else (pl.ds(0, 4) if e > 0 else pl.ds(4, 4))
                    move(name, needs, "x+" if e > 0 else "x-", (128 if k == 0 else 64) * KIB, dz, a, -e * k, half,
                         (e, 0, 0), rank=rank, drain=of_unit(dz, a))
                    arrived[dz, a].append(name)
        arrived[dz, a] += firsts + have
        if dz == 0:
            own_line = (firsts if a == 0 else own_line[0], firsts)

    for ez in (1, -1):
        link = "z+" if ez > 0 else "z-"
        lines = [(0, "own", own_line[0], 64, every, 0), (1, "own", own_line[1], 128, 0, every)]
        for way in (1, -1):
            for k in range(4):
                half = every if k < 3 else (pl.ds(0, 2) if way > 0 else pl.ds(2, 2))
                needs = [n for n in arrived[0, 0] if n.startswith(f"yl 0 0 {way} {k}")]
                lines.append((0, f"{way} {k}", needs, 64 if k < 3 else 32, half, -way * (k + 1)))
            for k in range(2):
                half = every if k < 1 else (pl.ds(0, 4) if way > 0 else pl.ds(4, 4))
                lines.append((1, f"{way} {k}", [f"xl 0 1 {way} {k}"], 128 if k < 1 else 64, -way * (k + 1), half))
        for a, label, needs, size, dx, dy in lines:
            name = f"zl {a} {ez} {label}"
            passes = a == (0 if ez > 0 else 1)
            as_one = {} if passes else dict(group=f"zl {a} {ez}", whole=lambda ez=ez, a=a: unit(-ez, a))
            move(name, needs, link, size * KIB, 0, a, dx, dy, (0, 0, ez), rank=RANKS.get(f"zl {a} {ez}", 2),
                 drain=(f"zl {ez}", lambda: blocks.at[0]), **as_one)
            arrived[-ez, a].append(name)
            if passes:
                further = f"zf {a} {ez} {label}"
                move(further, [name], link, size * KIB, -ez, a, dx, dy, (0, 0, ez), rank=RANKS.get(f"zf {ez}", 2), group=f"zf {ez}",
                     whole=lambda ez=ez, a=a: unit(-2 * ez, a), drain=("zf", lambda: blocks.at[0]))
                arrived[-2 * ez, a].append(further)

    def load(n):
        return lambda: loads[n].wait()

    for n in range(2):
        compute(f"load {n}", [], 0.6, load(n), rank=5)
        transfer(f"kv {n}", [f"load {n}"], "core", 1280 * KIB, lambda n=n: kv.at[n, c], lambda n=n: kv.at[n, c],
                 lambda n=n: kv.at[n, 1 - c], other_core, rank=9, drain=("kv", lambda: kv.at[:, c]))

    def key_norm():
        for half in range(2):
            def add(i, total):
                part = kv[0, half, :, pl.ds(pl.multiple_of(i * 128, 128), 128)].astype(F32)
                return total + part * part
            total = lax.fori_loop(0, D // 128, add, jnp.zeros((SL, 128), F32))
            norm[pl.ds(half * SL, SL), :] = jnp.broadcast_to(
                (0.5 * BETA) * jnp.sum(total, axis=1, keepdims=True), (SL, 128))

    compute("norm", ["load 0", "kv 0"], 1.1, key_norm, rank=6)

    def relayout(dz, a):
        def run():
            zz = (z + dz + NZ) % NZ
            for h in range(2):
                got = blocks[zz, a, 2 * h:2 * h + 2].reshape(256, F)
                laid = jnp.dot(spread[...], got, preferred_element_type=F32).astype(BF)
                for i in range(NF):
                    rows[a, zz % NDP, zz // NDP, pl.ds(32 * h, 32), i * F:(i + 1) * F] = laid[i * 32:(i + 1) * 32]
        return run

    for dz in range(-3, 5):
        for a in range(2):
            compute(f"rows {dz} {a}", arrived[dz, a], 0.12, relayout(dz, a), rank=3 if dz in (0, 4) else 8)

    def products(group):
        def one(n):
            return lax.dot_general(kv[n].reshape(2 * SL, D), rows[n, group].reshape(128, D), (((1,), (1,)), ((), ())),
                                   preferred_element_type=F32)
        return BETA * one(0) - norm[...], one(1)

    def own_scores():
        s, d = products(dp)
        scores[...] = s
        dprobs[...] = d
        top = jnp.max(s, axis=0, keepdims=True)
        e = jnp.exp(s - top)
        stat_y[y, 0:1] = top
        stat_y[y, 1:2] = jnp.sum(e, axis=0, keepdims=True)
        stat_y[y, 2:3] = jnp.sum(e * d, axis=0, keepdims=True)
        stat_y[y, 3:8] = jnp.zeros((5, 128), F32)

    def merge(ref):
        parts = [ref[i] for i in range(8)]
        top = parts[0][0:1]
        for p in parts[1:]:
            top = jnp.maximum(top, p[0:1])
        total = jnp.zeros((1, 128), F32)
        weighted = jnp.zeros((1, 128), F32)
        for p in parts:
            scale = jnp.exp(p[0:1] - top)
            total += p[1:2] * scale
            weighted += p[2:3] * scale
        return top, total, weighted

    compute("own scores", ["rows 0 0", "rows 0 1", "rows 4 0", "rows 4 1", "norm", "load 1", "kv 1"], 1.3, own_scores, rank=1)
    stats = ("stats", lambda: norm.at[pl.ds(0, 17 * 8)])
    for d in range(1, NY):
        transfer(f"sy {d}", ["own scores"], f"sy{d}", 4 * KIB, lambda: stat_y.at[y], lambda: stat_y.at[y],
                 lambda: stat_y.at[0], chip(0, d, 0), rank=-5,
                 group="sy", whole=lambda: stat_y.at[pl.ds(0, 7)], drain=stats)

    place = x * 2 + zh

    def merge_y():
        top, total, weighted = merge(stat_y)
        stat_x[place, 0:1] = top
        stat_x[place, 1:2] = total
        stat_x[place, 2:3] = weighted
        stat_x[place, 3:8] = jnp.zeros((5, 128), F32)

    compute("merge y", [f"sy {d}" for d in range(1, NY)], 0.3, merge_y, rank=0)
    for d in range(NX):
        for e in range(2):
            if d or e:
                transfer(f"sx {d} {e}", ["merge y"], f"sx{d}{e}", 4 * KIB, lambda: stat_x.at[place], lambda: stat_x.at[place],
                         lambda: stat_x.at[0], chip(d, 0, 4 * e), rank=-5,
                         group="sx", whole=lambda: stat_x.at[pl.ds(0, 7)], drain=stats)

    def merge_x():
        top, total, weighted = merge(stat_x)
        stat_f[dp, 0:1] = top + jnp.log(total)
        stat_f[dp, 1:2] = weighted / total
        stat_f[dp, 2:8] = jnp.zeros((6, 128), F32)

    compute("merge x", [f"sx {d} {e}" for d in range(NX) for e in range(2) if d or e], 0.3, merge_x, rank=0)
    for d in range(1, NDP):
        transfer(f"sf {d}", ["merge x"], f"sf{d}", 4 * KIB, lambda: stat_f.at[dp], lambda: stat_f.at[dp],
                 lambda: stat_f.at[0], {"dp": (dp + d) % NDP, "slot": slot}, rank=-5,
                 group="sf", whole=lambda: stat_f.at[pl.ds(0, 3)], drain=stats)

    def weights(group, s, d):
        lse = stat_f[group, 0:1]
        delta = stat_f[group, 1:2]
        prob = jnp.exp(s - lse)
        dscore = (BETA * prob * (d - delta)).astype(BF)
        probs[group] = prob.astype(BF).reshape(2, SL, 128)
        dscores[group] = dscore.reshape(2, SL, 128)
        return dscore

    def own_weights():
        dscore = weights(dp, scores[...], dprobs[...])
        turned[...] = dscore.astype(F32).T.astype(BF)

    def query_part(h):
        def part(i, _):
            cut = pl.ds(pl.multiple_of(i * F, F), F)
            out = jnp.dot(turned[...], kv[0, :, :, cut].reshape(2 * SL, F), preferred_element_type=F32)
            rs[:, :, :, cut] = out.astype(BF).reshape(2, NX, 16, F)
            return 0
        lax.fori_loop(h * NF // 2, (h + 1) * NF // 2, part, 0)

    compute("own weights", ["merge x"], 0.4, own_weights, rank=0)
    for h in range(2):
        compute(f"query part {h}", ["own weights"], 0.6, lambda h=h: query_part(h), rank=0)
    parts = ("parts", lambda: rs.at[:, pl.ds(0, 3)])
    low, high = slice(0, D // 2), slice(D // 2, D)
    for e, far, near in ((1, low, high), (-1, high, low)):
        link = "x+" if e > 0 else "x-"
        slot_in = 0 if e > 0 else 1
        transfer(f"ra {e}", [f"query part {0 if e > 0 else 1}"], link, 128 * KIB, lambda far=far: rs.at[:, (x + 2) % NX, :, far],
                 lambda s=slot_in: rs_a.at[s], lambda s=slot_in: rs_a.at[s], chip(e, 0, 0), rank=-2, drain=parts)
        transfer(f"rb {e} 0", [f"query part {1 if e > 0 else 0}"], link, 128 * KIB, lambda e=e, near=near: rs.at[:, (x + e + NX) % NX, :, near],
                 lambda s=slot_in, near=near: rs_x.at[s, :, :, near], lambda s=slot_in, near=near: rs_x.at[s, :, :, near],
                 chip(e, 0, 0), rank=-1, drain=parts)

        def add(e=e, far=far, slot_in=slot_in):
            to = (x + e + NX) % NX
            for i in range(NF // 2):
                cut = slice(far.start + i * F, far.start + (i + 1) * F)
                both = rs[:, to, :, cut].astype(F32) + rs_a[slot_in, :, :, i * F:(i + 1) * F].astype(F32)
                rs[:, to, :, cut] = both.astype(BF)

        compute(f"add {e}", [f"ra {e}"], 0.2, add, rank=0)
        transfer(f"rb {e} 1", [f"add {e}"], link, 128 * KIB, lambda e=e, far=far: rs.at[:, (x + e + NX) % NX, :, far],
                 lambda s=slot_in, far=far: rs_x.at[s, :, :, far], lambda s=slot_in, far=far: rs_x.at[s, :, :, far],
                 chip(e, 0, 0), rank=-1, drain=parts)

    def reduce_x():
        for i in range(NF):
            cut = slice(i * F, (i + 1) * F)
            total = rs[:, x, :, cut].astype(F32) + rs_x[0, :, :, cut].astype(F32) + rs_x[1, :, :, cut].astype(F32)
            rs_t[pl.ds(32 * i, 32), :] = total.reshape(32, F).astype(BF)
        laid = jnp.dot(gather_rows[...], rs_t[...], preferred_element_type=F32).astype(BF)
        rs_t[...] = laid

    compute("reduce x", [f"rb {e} {k}" for e in (1, -1) for k in range(2)], 0.6, reduce_x, rank=0)
    for d in range(1, NY):
        transfer(f"ry {d}", ["reduce x"], "y*" if d == 4 else "y+" if d < 4 else "y-", 32 * KIB,
                 lambda d=d: rs_t.at[pl.ds(pl.multiple_of(((y + d) % NY) * 32, 32), 32)],
                 lambda d=d: rs_y.at[d - 1], lambda d=d: rs_y.at[d - 1], chip(0, d, 0), hops=min(d, NY - d), rank=-3,
                 group="ry", whole=lambda: rs_y, drain=("ry", lambda: rs_y))

    def reduce_y():
        total = rs_t[pl.ds(pl.multiple_of(y * 32, 32), 32), :].astype(F32)
        for d in range(NY - 1):
            total += rs_y[d].astype(F32)
        rs_z[0:2] = total.astype(BF).reshape(2, 16, F)

    compute("reduce y", [f"ry {d}" for d in range(1, NY)], 0.3, reduce_y, rank=0)
    transfer("rz", ["reduce y"], "z*", 16 * KIB, lambda: rs_z.at[1 - zh], lambda: rs_z.at[2], lambda: rs_z.at[2],
             chip(0, 0, 4), hops=4, rank=-3, drain=of_unit(0, 1))

    def finish_queries():
        total = rs_z[zh].astype(F32) + rs_z[2].astype(F32)
        lines = [jnp.concatenate([total[8 * r + i:8 * r + i + 1] for i in range(NF)], axis=1) for r in range(2)]
        qg_ref[...] = jnp.concatenate(lines, axis=0)

    compute("finish queries", ["rz"], 0.2, finish_queries, rank=12)

    def other_group(k):
        def run():
            group = (dp + k) % NDP
            s, d = products(group)
            weights(group, s, d)
        return run

    for k in range(1, NDP):
        zs = [k, k - 4]
        compute(f"group {k}", [f"rows {d} {a}" for d in zs for a in range(2)] + [f"sf {NDP - k}", "norm", "load 1", "kv 1"],
                1.3, other_group(k), rank=7)

    def gradients(core, j, store):
        left_k = jnp.concatenate([dscores[i, core] for i in range(NDP)], axis=1)
        left_v = jnp.concatenate([probs[i, core] for i in range(NDP)], axis=1)
        column = jnp.sum(left_k.astype(F32), axis=1, keepdims=True)
        for i in range(j * NF // PIECES, (j + 1) * NF // PIECES):
            cut = slice(i * F, (i + 1) * F)
            grad = jnp.dot(left_k, rows[0, :, :, :, cut].reshape(512, F), preferred_element_type=F32)
            store(i, 0, grad - column * kv[0, core, :, cut].astype(F32))
            store(i, 1, jnp.dot(left_v, rows[1, :, :, :, cut].reshape(512, F), preferred_element_type=F32))

    groups = [f"group {k}" for k in range(1, NDP)] + ["own weights"]
    wide = D // PIECES

    def store_in(ref):
        def store(i, n, value):
            ref[n, :, i * F:(i + 1) * F] = value.astype(BF)
        return store

    def storing(j, n):
        cut = pl.ds(j * wide, wide)
        return pltpu.make_async_copy(own.at[n, :, cut], (ownv_hbm if n else ownk_hbm).at[:, cut], store_sem)

    def own_part(j):
        gradients(c, j, store_in(own))
        for n in range(2):
            storing(j, n).start()

    for j in range(PIECES):
        cut = pl.ds(j * wide, wide)
        compute(f"other {j}", groups, 0.3, lambda j=j: gradients(1 - c, j, store_in(cross)), rank=20)
        for n, ref in enumerate((crossk_hbm, crossv_hbm)):
            transfer(f"cx {j} {n}", [f"other {j}"], "core", SL * wide * 2, lambda n=n, cut=cut: cross.at[n, :, cut],
                     lambda ref=ref, cut=cut: ref.at[:, cut], lambda ref=ref: ref, other_core, rank=0,
                     group=f"cx {n}", whole=lambda ref=ref: ref, drain=("cx", lambda: cross))
        compute(f"own {j}", groups, 0.3, lambda j=j: own_part(j), rank=21)

    assert len(recv_index) <= RECEIVES and len(send_index) <= SENDS
    for what, name in plan.order():
        if what == "start":
            emit[name][0]().start()
        elif what == "wait":
            emit[name][1]().wait_recv()
        else:
            emit[name]()

    for view, n, peer, size in sent.values():
        ref = view()
        assert math.prod(ref.shape) * jnp.dtype(ref.dtype).itemsize == size
        pltpu.make_async_remote_copy(
            src_ref=ref, dst_ref=ref, send_sem=send_sem.at[n], recv_sem=recv_sem.at[0],
            device_id=peer, device_id_type=MESH).wait_send()
    pltpu.make_async_copy(own, own, store_sem).wait()


PIECES = 4
def add_halves(query, own_k, own_v, cross_k, cross_v, query_out, key_out, value_out, parts, sums, in_sem, out_sem):
    def coming(n, h):
        cut = pl.ds(h * SL // 2, SL // 2)
        return pltpu.make_async_copy((own_k, cross_k, own_v, cross_v)[n].at[cut], parts.at[n, cut], in_sem.at[n, h])

    def going(n, h):
        cut = pl.ds(h * SL // 2, SL // 2)
        return pltpu.make_async_copy(sums.at[n, cut], (key_out, value_out)[n].at[cut], out_sem.at[n, h])

    order = [(n, h) for h in range(2) for n in range(2)]
    for n, h in order:
        coming(2 * n, h).start()
        coming(2 * n + 1, h).start()
    query_out[...] = query[...].astype(BF)
    for n, h in order:
        coming(2 * n, h).wait()
        coming(2 * n + 1, h).wait()
        cut = pl.ds(h * SL // 2, SL // 2)
        sums[n, cut] = (parts[2 * n, cut].astype(F32) + parts[2 * n + 1, cut].astype(F32)).astype(BF)
        going(n, h).start()
    for n, h in order:
        going(n, h).wait()


SENDS = 19
RECEIVES = 150


def body(queries, keys, values, cotangent):
    vmem = pl.BlockSpec(memory_space=pltpu.VMEM)
    hbm = pl.BlockSpec(memory_space=pl.ANY)
    query, own_k, own_v, cross_k, cross_v = pl.pallas_call(
        kernel,
        name="memory_backward",
        out_shape=(
            jax.ShapeDtypeStruct((2, D), F32),
            *[jax.ShapeDtypeStruct((SL, D), BF)] * 4,
        ),
        in_specs=[vmem, vmem, hbm, hbm],
        out_specs=(vmem, hbm, hbm, hbm, hbm),
        scratch_shapes=[
            pltpu.VMEM((NZ, 2, NX, NY, 16, F), BF),
            pltpu.VMEM((2, NDP, 2, 64, D), BF),
            pltpu.VMEM((2, 2, SL, D), BF),
            pltpu.VMEM((2 * SL, 128), F32),
            pltpu.VMEM((256, 256), BF),
            pltpu.VMEM((256, 256), BF),
            pltpu.VMEM((128, 2 * SL), BF),
            pltpu.VMEM((NDP, 2, SL, 128), BF),
            pltpu.VMEM((NDP, 2, SL, 128), BF),
            pltpu.VMEM((2 * SL, 128), F32),
            pltpu.VMEM((2 * SL, 128), F32),
            pltpu.VMEM((NY, 8, 128), F32),
            pltpu.VMEM((2 * NX, 8, 128), F32),
            pltpu.VMEM((NDP, 8, 128), F32),
            pltpu.VMEM((2, NX, 16, D), BF),
            pltpu.VMEM((2, 2, 16, D // 2), BF),
            pltpu.VMEM((2, 2, 16, D), BF),
            pltpu.VMEM((256, F), BF),
            pltpu.VMEM((NY - 1, 32, F), BF),
            pltpu.VMEM((3, 16, F), BF),
            pltpu.VMEM((2, SL, D), BF),
            pltpu.VMEM((2, SL, D), BF),
            pltpu.SemaphoreType.DMA((SENDS,)),
            pltpu.SemaphoreType.DMA((RECEIVES,)),
            pltpu.SemaphoreType.DMA((2,)),
            pltpu.SemaphoreType.DMA,
        ],
        compiler_params=pltpu.CompilerParams(
            collective_id=0, has_side_effects=True, vmem_limit_bytes=56 * 2**20
        ),
    )(queries, cotangent, keys, values)
    return pl.pallas_call(
        add_halves,
        name="add_halves",
        out_shape=(jax.ShapeDtypeStruct((2, D), BF), *[jax.ShapeDtypeStruct((SL, D), BF)] * 2),
        in_specs=[vmem, hbm, hbm, hbm, hbm],
        out_specs=(vmem, hbm, hbm),
        scratch_shapes=[
            pltpu.VMEM((4, SL, D), BF),
            pltpu.VMEM((2, SL, D), BF),
            pltpu.SemaphoreType.DMA((4, 2)),
            pltpu.SemaphoreType.DMA((2, 2)),
        ],
        compiler_params=pltpu.CompilerParams(vmem_limit_bytes=24 * 2**20),
    )(query, own_k, own_v, cross_k, cross_v)


def solution(mesh):
    rows = P(("dp", "slot"), None)
    slots = P("slot", None)
    return jax.shard_map(
        body,
        mesh=mesh,
        in_specs=(rows, slots, slots, rows),
        out_specs=(rows, slots, slots),
        check_vma=False,
    )
```

```python
import math

import jax
import jax.numpy as jnp
from jax import lax
from jax.experimental import pallas as pl
from jax.experimental.pallas import tpu as pltpu
from jax.sharding import PartitionSpec as P

MESH = pl.DeviceIdType.MESH
D = 4096
BETA = 1.25 * D ** (-0.5)
NX, NY, NZ, NDP = 4, 8, 8, 4
SL = 160
F = 512
NF = D // F
BF = jnp.bfloat16
F32 = jnp.float32


UNITS = (
    (0, 0, "xy"),
    (0, 1, "yx"),
    (4, 0, "xy"),
    (4, 1, "yx"),
    (3, 0, "xy"),
    (3, 1, "yx"),
    (-3, 0, "xy"),
    (-3, 1, "yx"),
    (2, 0, "xy"),
    (-2, 1, "yx"),
)
RANKS = {
    "first": {(-3, 0): 6, (-3, 1): 0, (-2, 1): 0.5, (0, 0): 0, (0, 1): 6, (2, 0): 6, (3, 0): 1, (3, 1): 2, (4, 0): 7, (4, 1): 3},
    "line": {(-3, 0): 7, (-3, 1): 5, (-2, 1): 0, (0, 0): 3, (0, 1): 8, (2, 0): 8, (3, 0): 4, (3, 1): 2, (4, 0): 0, (4, 1): 0.5},
    "z1": {(-3, 0): 3, (-3, 1): 5, (-2, 0): 4, (2, 1): 4, (3, 0): 2, (3, 1): 4, (4, 0): 1, (4, 1): 2},
    "zf": {(-1, 0): 5, (1, 0): 7},
    "zl": {(-1, 0): 5, (-1, 1): 2, (1, 0): 4, (1, 1): 0.5},
}


def rank_of(kind, offset, array):
    return RANKS.get(kind, {}).get((offset, array), 1)


HOP_US = 2.3
FAR_US = 0.4
CORE_HOP_US = 1.5
LINK_RATE = 48e3
CORE_RATE = 500e3
BACKLOG_US = 0.7
START_US = 0.05
WAIT_US = 0.03


class Plan:
    def __init__(self):
        self.items = {}

        self.members = {}

    def transfer(self, name, needs, link, size, hops=1, rank=0, group=None):
        group = group or name
        self.members.setdefault(group, []).append(name)
        self.items[name] = dict(kind="t", needs=list(needs), link=link, size=size, hops=hops, rank=rank, group=group)

    def compute(self, name, needs, cost, rank=0):
        self.items[name] = dict(kind="c", needs=list(needs), cost=cost, rank=rank)

    def order(self):
        now = 0.0
        done, started, landing, arrivals, free, steps = set(), set(), {}, {}, {}, []
        group_of = {n: i.get("group", n) for n, i in self.items.items()}
        needs = {n: {group_of[d] for d in i["needs"]} for n, i in self.items.items()}
        left = set(group_of.values())
        while left:
            ready = [n for n in self.items if n not in started and needs[n] <= done]
            held = []
            sends = sorted((n for n in ready if self.items[n]["kind"] == "t"), key=lambda n: self.items[n]["rank"])
            for n in sends:
                i = self.items[n]
                rate, hop = (CORE_RATE, CORE_HOP_US) if i["link"] == "core" else (LINK_RATE, HOP_US)
                links = [i["link"][0] + w for w in "+-"] if i["link"].endswith("*") else [i["link"]]
                queued = max(free.get(link, 0.0) for link in links)
                if queued - now > BACKLOG_US and i["rank"] > 0:
                    held.append(queued - BACKLOG_US)
                    continue
                now += START_US
                for link in links:
                    free[link] = max(now, free.get(link, 0.0)) + i["size"] * i["hops"] / rate / len(links)
                landing[n] = max(free[link] for link in links) + hop + FAR_US * (i["hops"] - 1)
                started.add(n)
                steps.append(("start", n))
                group = i["group"]
                if all(m in started for m in self.members[group]):
                    arrivals[group] = max(landing[m] for m in self.members[group])
            first = min(arrivals, key=lambda n: (arrivals[n], str(n))) if arrivals else None
            if first is not None and arrivals[first] <= now:
                steps.append(("wait", first))
                arrivals.pop(first)
                done.add(first)
                left.discard(first)
                now += WAIT_US
                continue
            runs = sorted((n for n in ready if self.items[n]["kind"] == "c"), key=lambda n: self.items[n]["rank"])
            if runs:
                n = runs[0]
                now += self.items[n]["cost"]
                started.add(n)
                done.add(n)
                left.discard(n)
                steps.append(("run", n))
                continue
            if held and (first is None or min(held) < arrivals[first]):
                now = max(now, min(held)) + 0.001
                continue
            now = max(now, arrivals.pop(first)) + WAIT_US
            steps.append(("wait", first))
            done.add(first)
            left.discard(first)
        self.end = now
        return steps


def kernel(q_ref, g_ref, k_hbm, v_hbm, qg_ref, kg_ref, vg_ref,
           blocks, rows, kv, norm, spread, gather_rows, turned, probs, dscores, scores, dprobs,
           stat_y, stat_x, stat_f, rs, rs_a, rs_x, rs_t, rs_y, rs_z, own, cross, landed,
           send_sem, recv_sem, load_sem):
    dp = lax.axis_index("dp")
    slot = lax.axis_index("slot")
    c = slot % 2
    y = (slot // 2) % NY
    zh = (slot // 16) % 2
    x = slot // 32
    z = zh * NDP + dp

    def chip(dx, dy, dz):
        zz = (z + dz + NZ) % NZ
        return {"dp": zz % NDP, "slot": ((((x + dx + NX) % NX) * 2 + zz // NDP) * NY + (y + dy + NY) % NY) * 2 + c}

    other_core = {"dp": dp, "slot": slot + 1 - 2 * c}

    loads = []
    for n, src in enumerate((k_hbm, v_hbm)):
        cp = pltpu.make_async_copy(src, kv.at[n, c], load_sem.at[n])
        cp.start()
        loads.append(cp)

    barrier = pltpu.get_barrier_semaphore()
    peers = [chip(d, 0, 0) for d in range(1, NX)] + [chip(0, d, 0) for d in range(1, NY)]
    peers += [chip(0, 0, d) for d in range(1, NZ)] + [chip(d, 0, 4) for d in range(1, NX)] + [other_core]
    for p in peers:
        pl.semaphore_signal(barrier, inc=1, device_id=p, device_id_type=MESH)

    def to_rows16(ref):
        wide = ref[...].astype(F32)
        return jnp.concatenate([wide[r:r + 1, i * F:(i + 1) * F] for r in range(2) for i in range(NF)], axis=0).astype(BF)

    blocks[z, 0, x, y] = to_rows16(q_ref)
    blocks[z, 1, x, y] = to_rows16(g_ref)

    row = lax.broadcasted_iota(jnp.int32, (256, 256), 0)
    col = lax.broadcasted_iota(jnp.int32, (256, 256), 1)
    spread[...] = jnp.where(col == (row % 32) * NF + row // 32, 1.0, 0.0).astype(BF)
    want = (row % 8) * 32 + ((row // 16) % 2) * 16 + (row // 32) * 2 + (row // 8) % 2
    gather_rows[...] = jnp.where(col == want, 1.0, 0.0).astype(BF)

    pl.semaphore_wait(barrier, len(peers))

    plan = Plan()
    emit = {}
    send_index = {}
    recv_index = {}
    sent = {}

    def transfer(name, needs, link, size, src, dst, incoming, peer, hops=1, rank=0, group=None, whole=None, drain=None):
        plan.transfer(name, needs, link, size, hops, rank, group)
        r = recv_index.setdefault(group or name, len(recv_index))
        key, view = drain or (name, src)
        n = send_index.setdefault(key, len(send_index))
        if size:
            sent.setdefault(key, [view, n, peer, 0])[3] += size

        def out():
            return pltpu.make_async_remote_copy(
                src_ref=src(), dst_ref=dst(), send_sem=send_sem.at[n], recv_sem=recv_sem.at[r],
                device_id=peer, device_id_type=MESH)

        def into():
            ref = (whole or incoming)()
            return pltpu.make_async_remote_copy(
                src_ref=ref, dst_ref=ref, send_sem=send_sem.at[n], recv_sem=recv_sem.at[r],
                device_id=peer, device_id_type=MESH)

        emit[name] = (out, into)
        if group:
            emit[group] = (out, into)

    def compute(name, needs, cost, run, rank=0):
        plan.compute(name, needs, cost, rank)
        emit[name] = run

    def at(dz, a, dx, dy):
        xs = dx if not isinstance(dx, int) else (x + dx + NX) % NX
        ys = dy if not isinstance(dy, int) else (y + dy + NY) % NY
        return blocks.at[(z + dz + NZ) % NZ, a, xs, ys]

    def unit(dz, a):
        return blocks.at[(z + dz + NZ) % NZ, a]

    def move(name, needs, link, size, dz, a, dx, dy, step, hops=1, rank=0, **names):
        ex, ey, ez = step

        def shifted(d, e):
            return d if not isinstance(d, int) else d - e

        transfer(name, needs, link, size, lambda: at(dz, a, dx, dy), lambda: at(dz, a, dx, dy),
                 lambda: at(dz - ez, a, shifted(dx, ex), shifted(dy, ey)), chip(*step), hops, rank, **names)

    KIB = 1024
    every = slice(None)

    def of_unit(dz, a, part=None):
        if dz == 0 and a == 0:
            if part == "xp":
                return "own xp", lambda: blocks.at[0, 0, 0, pl.ds(0, 3)]
            return "own yl", lambda: blocks.at[0, 0, :, pl.ds(0, 7)]
        return ("unit", dz, a,), lambda: unit(dz, a)

    for ez, a in ((4, 0), (4, 1), (-3, 0), (3, 0), (-3, 1), (3, 1), (-2, 0), (2, 1)):
        move(("z1", ez, a,), [], "z*" if ez == 4 else "z+" if ez > 0 else "z-", 16 * KIB, 0, a, 0, 0, (0, 0, ez),
             hops=abs(ez), rank=rank_of("z1", ez, a), drain=of_unit(4 if ez == 4 else -ez, a))

    def first_hop(dz, a):
        return [] if dz == 0 else [("z1", 4, a,) if dz == 4 else ("z1", -dz, a,)]

    def line_parts(dz):
        return (0, 1) if dz in (0, 4) else (None,)

    arrived = {(dz, a): [] for dz in range(-3, 5) for a in range(2)}
    for u, (dz, a, route) in enumerate(UNITS):
        have = first_hop(dz, a)
        near = dz in (0, 4)
        first, rank = rank_of("first", dz, a), rank_of("line", dz, a)
        firsts = []
        if route == "xy":
            for e in (1, -1, 2):
                name = ("xp", dz, a, e,)
                move(name, have, "x*" if e == 2 else "x-" if e < 0 else "x+", 16 * KIB, dz, a, 0, 0, (e, 0, 0), hops=abs(e), rank=first,
                     group=("xp", dz, a,), whole=lambda: blocks.at[0, 0, 0, pl.ds(0, 3)], drain=of_unit(dz, a, "xp"))
                firsts.append(name)
            for k in range(4):
                for way in (1, -1):
                    for h in line_parts(dz):
                        if k == 3 and h == (1 if way > 0 else 0):
                            continue
                        needs = firsts + have if k == 0 else [("yl", dz, a, way, k - 1, h,)]
                        half = (pl.ds(0, 2) if way > 0 else pl.ds(2, 2)) if k == 3 else every if h is None else pl.ds(2 * h, 2)
                        name = ("yl", dz, a, way, k, h,)
                        move(name, needs, "y+" if way > 0 else "y-", (64 if k < 3 and h is None else 32) * KIB,
                             dz, a, half, -way * k, (0, way, 0), rank=rank, drain=of_unit(dz, a))
                        arrived[dz, a].append(name)
        else:
            if near:
                for d in range(1, NY):
                    name = ("yp", dz, a, d,)
                    move(name, have, "y*" if d == 4 else "y+" if d < 4 else "y-", 16 * KIB, dz, a, 0, 0, (0, d, 0), hops=min(d, NY - d), rank=first,
                         group=("yp", dz, a,), whole=lambda: blocks.at[0, 0, 0, pl.ds(0, 7)], drain=of_unit(dz, a))
                    firsts.append(name)
            else:
                for way in (1, -1):
                    for k in range(4 if (way > 0) == (u % 4 == 1) else 3):
                        name = ("yp", dz, a, way, k,)
                        needs = have if k == 0 else [("yp", dz, a, way, k - 1,)]
                        move(name, needs, "y+" if way > 0 else "y-", 16 * KIB, dz, a, 0, -way * k, (0, way, 0), rank=first,
                             drain=of_unit(dz, a))
                        firsts.append(name)
            for e in (1, -1):
                for k in range(2):
                    needs = firsts + have if k == 0 else [("xl", dz, a, e, 0,)]
                    name = ("xl", dz, a, e, k,)
                    half = every if k == 0 else (pl.ds(0, 4) if e > 0 else pl.ds(4, 4))
                    move(name, needs, "x+" if e > 0 else "x-", (128 if k == 0 else 64) * KIB, dz, a, -e * k, half,
                         (e, 0, 0), rank=rank, drain=of_unit(dz, a))
                    arrived[dz, a].append(name)
        arrived[dz, a] += firsts + have
        if dz == 0:
            own_line = (firsts if a == 0 else own_line[0], firsts)

    for ez in (1, -1):
        link = "z+" if ez > 0 else "z-"
        lines = [(0, ("own",), own_line[0], 64, every, 0), (1, ("own",), own_line[1], 128, 0, every)]
        for way in (1, -1):
            for k in range(4):
                half = every if k < 3 else (pl.ds(0, 2) if way > 0 else pl.ds(2, 2))
                needs = [n for n in arrived[0, 0] if n[:5] == ("yl", 0, 0, way, k)]
                lines.append((0, (way, k), needs, 64 if k < 3 else 32, half, -way * (k + 1)))
            for k in range(2):
                half = every if k < 1 else (pl.ds(0, 4) if way > 0 else pl.ds(4, 4))
                lines.append((1, (way, k), [("xl", 0, 1, way, k,)], 128 if k < 1 else 64, -way * (k + 1), half))
        for a, label, needs, size, dx, dy in lines:
            name = ("zl", a, ez, *label)
            passes = a == (0 if ez > 0 else 1)
            as_one = {} if passes else dict(group=("zl", a, ez,), whole=lambda ez=ez, a=a: unit(-ez, a))
            move(name, needs, link, size * KIB, 0, a, dx, dy, (0, 0, ez), rank=rank_of("zl", ez, a),
                 drain=(("zl", ez,), lambda: blocks.at[0]), **as_one)
            arrived[-ez, a].append(name)
            if passes:
                further = ("zf", a, ez, *label)
                move(further, [name], link, size * KIB, -ez, a, dx, dy, (0, 0, ez), rank=rank_of("zf", ez, 0), group=("zf", ez,),
                     whole=lambda ez=ez, a=a: unit(-2 * ez, a), drain=("zf", lambda: blocks.at[0]))
                arrived[-2 * ez, a].append(further)

    def load(n):
        return lambda: loads[n].wait()

    for n in range(2):
        compute(("load", n,), [], 0.6, load(n), rank=5)
        transfer(("kv", n,), [("load", n,)], "core", 1280 * KIB, lambda n=n: kv.at[n, c], lambda n=n: kv.at[n, c],
                 lambda n=n: kv.at[n, 1 - c], other_core, rank=9, drain=("kv", lambda: kv.at[:, c]))

    def key_norm():
        for half in range(2):
            def add(i, total):
                part = kv[0, half, :, pl.ds(pl.multiple_of(i * 128, 128), 128)].astype(F32)
                return total + part * part
            total = lax.fori_loop(0, D // 128, add, jnp.zeros((SL, 128), F32))
            norm[pl.ds(half * SL, SL), :] = jnp.broadcast_to(
                (0.5 * BETA) * jnp.sum(total, axis=1, keepdims=True), (SL, 128))

    compute("norm", [("load", 0), ("kv", 0)], 1.1, key_norm, rank=6)

    def relayout(dz, a):
        def run():
            zz = (z + dz + NZ) % NZ
            for h in range(2):
                got = blocks[zz, a, 2 * h:2 * h + 2].reshape(256, F)
                laid = jnp.dot(spread[...], got, preferred_element_type=F32).astype(BF)
                for i in range(NF):
                    rows[a, zz % NDP, zz // NDP, pl.ds(32 * h, 32), i * F:(i + 1) * F] = laid[i * 32:(i + 1) * 32]
        return run

    for dz in range(-3, 5):
        for a in range(2):
            compute(("rows", dz, a,), arrived[dz, a], 0.12, relayout(dz, a), rank=3 if dz in (0, 4) else 8)

    def products(group):
        def one(n):
            return lax.dot_general(kv[n].reshape(2 * SL, D), rows[n, group].reshape(128, D), (((1,), (1,)), ((), ())),
                                   preferred_element_type=F32)
        return BETA * one(0) - norm[...], one(1)

    def own_scores():
        s, d = products(dp)
        scores[...] = s
        dprobs[...] = d
        top = jnp.max(s, axis=0, keepdims=True)
        e = jnp.exp(s - top)
        stat_y[y, 0:1] = top
        stat_y[y, 1:2] = jnp.sum(e, axis=0, keepdims=True)
        stat_y[y, 2:3] = jnp.sum(e * d, axis=0, keepdims=True)
        stat_y[y, 3:8] = jnp.zeros((5, 128), F32)

    def merge(ref):
        parts = [ref[i] for i in range(8)]
        top = parts[0][0:1]
        for p in parts[1:]:
            top = jnp.maximum(top, p[0:1])
        total = jnp.zeros((1, 128), F32)
        weighted = jnp.zeros((1, 128), F32)
        for p in parts:
            scale = jnp.exp(p[0:1] - top)
            total += p[1:2] * scale
            weighted += p[2:3] * scale
        return top, total, weighted

    compute("own scores", [("rows", 0, 0), ("rows", 0, 1), ("rows", 4, 0), ("rows", 4, 1), "norm", ("load", 1), ("kv", 1)], 1.3, own_scores, rank=1)
    stats = ("stats", lambda: norm.at[pl.ds(0, 17 * 8)])
    for d in range(1, NY):
        transfer(("sy", d,), ["own scores"], "s", 4 * KIB, lambda: stat_y.at[y], lambda: stat_y.at[y],
                 lambda: stat_y.at[0], chip(0, d, 0), rank=-5,
                 group="sy", whole=lambda: stat_y.at[pl.ds(0, 7)], drain=stats)

    place = x * 2 + zh

    def merge_y():
        top, total, weighted = merge(stat_y)
        stat_x[place, 0:1] = top
        stat_x[place, 1:2] = total
        stat_x[place, 2:3] = weighted
        stat_x[place, 3:8] = jnp.zeros((5, 128), F32)

    compute("merge y", [("sy", d,) for d in range(1, NY)], 0.3, merge_y, rank=0)
    for d in range(NX):
        for e in range(2):
            if d or e:
                transfer(("sx", d, e,), ["merge y"], "s", 4 * KIB, lambda: stat_x.at[place], lambda: stat_x.at[place],
                         lambda: stat_x.at[0], chip(d, 0, 4 * e), rank=-5,
                         group="sx", whole=lambda: stat_x.at[pl.ds(0, 7)], drain=stats)

    def merge_x():
        top, total, weighted = merge(stat_x)
        stat_f[dp, 0:1] = top + jnp.log(total)
        stat_f[dp, 1:2] = weighted / total
        stat_f[dp, 2:8] = jnp.zeros((6, 128), F32)

    compute("merge x", [("sx", d, e,) for d in range(NX) for e in range(2) if d or e], 0.3, merge_x, rank=0)
    for d in range(1, NDP):
        transfer(("sf", d,), ["merge x"], "s", 4 * KIB, lambda: stat_f.at[dp], lambda: stat_f.at[dp],
                 lambda: stat_f.at[0], {"dp": (dp + d) % NDP, "slot": slot}, rank=-5,
                 group="sf", whole=lambda: stat_f.at[pl.ds(0, 3)], drain=stats)

    def weights(group, s, d):
        lse = stat_f[group, 0:1]
        delta = stat_f[group, 1:2]
        prob = jnp.exp(s - lse)
        dscore = (BETA * prob * (d - delta)).astype(BF)
        probs[group] = prob.astype(BF).reshape(2, SL, 128)
        dscores[group] = dscore.reshape(2, SL, 128)
        return dscore

    def own_weights():
        dscore = weights(dp, scores[...], dprobs[...])
        turned[...] = dscore.astype(F32).T.astype(BF)

    def query_part(h):
        def part(i, _):
            cut = pl.ds(pl.multiple_of(i * F, F), F)
            out = jnp.dot(turned[...], kv[0, :, :, cut].reshape(2 * SL, F), preferred_element_type=F32)
            rs[:, :, :, cut] = out.astype(BF).reshape(2, NX, 16, F)
            return 0
        lax.fori_loop(h * NF // 2, (h + 1) * NF // 2, part, 0)

    compute("own weights", ["merge x"], 0.4, own_weights, rank=0)
    for h in range(2):
        compute(("query", "part", h,), ["own weights"], 0.6, lambda h=h: query_part(h), rank=0)
    parts = ("parts", lambda: rs.at[:, pl.ds(0, 3)])
    low, high = slice(0, D // 2), slice(D // 2, D)
    for e, far, near in ((1, low, high), (-1, high, low)):
        link = "x+" if e > 0 else "x-"
        slot_in = 0 if e > 0 else 1
        transfer(("ra", e,), [("query", "part", 0 if e > 0 else 1,)], link, 128 * KIB, lambda far=far: rs.at[:, (x + 2) % NX, :, far],
                 lambda s=slot_in: rs_a.at[s], lambda s=slot_in: rs_a.at[s], chip(e, 0, 0), rank=-2, drain=parts)
        transfer(("rb", e, 0,), [("query", "part", 1 if e > 0 else 0,)], link, 128 * KIB, lambda e=e, near=near: rs.at[:, (x + e + NX) % NX, :, near],
                 lambda s=slot_in, near=near: rs_x.at[s, :, :, near], lambda s=slot_in, near=near: rs_x.at[s, :, :, near],
                 chip(e, 0, 0), rank=-1, drain=parts)

        def add(e=e, far=far, slot_in=slot_in):
            to = (x + e + NX) % NX
            for i in range(NF // 2):
                cut = slice(far.start + i * F, far.start + (i + 1) * F)
                both = rs[:, to, :, cut].astype(F32) + rs_a[slot_in, :, :, i * F:(i + 1) * F].astype(F32)
                rs[:, to, :, cut] = both.astype(BF)

        compute(("add", e,), [("ra", e,)], 0.2, add, rank=0)
        transfer(("rb", e, 1,), [("add", e,)], link, 128 * KIB, lambda e=e, far=far: rs.at[:, (x + e + NX) % NX, :, far],
                 lambda s=slot_in, far=far: rs_x.at[s, :, :, far], lambda s=slot_in, far=far: rs_x.at[s, :, :, far],
                 chip(e, 0, 0), rank=-1, drain=parts)

    def reduce_x():
        for i in range(NF):
            cut = slice(i * F, (i + 1) * F)
            total = rs[:, x, :, cut].astype(F32) + rs_x[0, :, :, cut].astype(F32) + rs_x[1, :, :, cut].astype(F32)
            rs_t[pl.ds(32 * i, 32), :] = total.reshape(32, F).astype(BF)
        laid = jnp.dot(gather_rows[...], rs_t[...], preferred_element_type=F32).astype(BF)
        rs_t[...] = laid

    compute("reduce x", [("rb", e, k,) for e in (1, -1) for k in range(2)], 0.6, reduce_x, rank=0)
    for d in range(1, NY):
        transfer(("ry", d,), ["reduce x"], "y*" if d == 4 else "y+" if d < 4 else "y-", 32 * KIB,
                 lambda d=d: rs_t.at[pl.ds(pl.multiple_of(((y + d) % NY) * 32, 32), 32)],
                 lambda d=d: rs_y.at[d - 1], lambda d=d: rs_y.at[d - 1], chip(0, d, 0), hops=min(d, NY - d), rank=-3,
                 group="ry", whole=lambda: rs_y, drain=("ry", lambda: rs_y))

    def reduce_y():
        total = rs_t[pl.ds(pl.multiple_of(y * 32, 32), 32), :].astype(F32)
        for d in range(NY - 1):
            total += rs_y[d].astype(F32)
        rs_z[0:2] = total.astype(BF).reshape(2, 16, F)

    compute("reduce y", [("ry", d,) for d in range(1, NY)], 0.3, reduce_y, rank=0)
    transfer("rz", ["reduce y"], "z*", 16 * KIB, lambda: rs_z.at[1 - zh], lambda: rs_z.at[2], lambda: rs_z.at[2],
             chip(0, 0, 4), hops=4, rank=-3, drain=of_unit(0, 1))

    def finish_queries():
        total = rs_z[zh].astype(F32) + rs_z[2].astype(F32)
        lines = [jnp.concatenate([total[8 * r + i:8 * r + i + 1] for i in range(NF)], axis=1) for r in range(2)]
        qg_ref[...] = jnp.concatenate(lines, axis=0).astype(BF)

    compute("finish queries", ["rz"], 0.2, finish_queries, rank=12)

    def other_group(k):
        def run():
            group = (dp + k) % NDP
            s, d = products(group)
            weights(group, s, d)
        return run

    for k in range(1, NDP):
        zs = [k, k - 4]
        compute(("group", k,), [("rows", d, a,) for d in zs for a in range(2)] + [("sf", NDP - k,), "norm", ("load", 1), ("kv", 1)],
                1.3, other_group(k), rank=7)

    def gradients(core, j, store):
        left_k = jnp.concatenate([dscores[i, core] for i in range(NDP)], axis=1)
        left_v = jnp.concatenate([probs[i, core] for i in range(NDP)], axis=1)
        column = jnp.sum(left_k.astype(F32), axis=1, keepdims=True)
        for i in range(j * NF // PIECES, (j + 1) * NF // PIECES):
            cut = slice(i * F, (i + 1) * F)
            grad = jnp.dot(left_k, rows[0, :, :, :, cut].reshape(512, F), preferred_element_type=F32)
            store(i, 0, grad - column * kv[0, core, :, cut].astype(F32))
            store(i, 1, jnp.dot(left_v, rows[1, :, :, :, cut].reshape(512, F), preferred_element_type=F32))

    groups = [("group", k) for k in range(1, NDP)] + ["own weights"]
    wide = D // PIECES

    def store_in(ref):
        def store(i, n, value):
            ref[n, :, i * F:(i + 1) * F] = value.astype(ref.dtype)
        return store

    def finish(j):
        for i in range(j * NF // PIECES, (j + 1) * NF // PIECES):
            cut = slice(i * F, (i + 1) * F)
            for n, ref in enumerate((kg_ref, vg_ref)):
                ref[:, cut] = (own[n, :, cut] + landed[n, :, cut].astype(F32)).astype(BF)

    for j in range(PIECES):
        cut = pl.ds(j * wide, wide)
        compute(("other", j), groups, 0.3, lambda j=j: gradients(1 - c, j, store_in(cross)), rank=20)
        transfer(("cx", j), [("other", j)], "core", 2 * SL * wide * 2, lambda cut=cut: cross.at[:, :, cut],
                 lambda cut=cut: landed.at[:, :, cut], lambda cut=cut: landed.at[:, :, cut], other_core, rank=0,
                 drain=("cx", lambda: cross))
        compute(("own", j), groups, 0.3, lambda j=j: gradients(c, j, store_in(own)), rank=21)
        compute(("finish", j), [("own", j), ("cx", j)], 0.2, lambda j=j: finish(j), rank=22)

    assert len(recv_index) <= RECEIVES and len(send_index) <= SENDS
    for what, name in plan.order():
        if what == "start":
            emit[name][0]().start()
        elif what == "wait":
            emit[name][1]().wait_recv()
        else:
            emit[name]()

    for view, n, peer, size in sent.values():
        ref = view()
        assert math.prod(ref.shape) * jnp.dtype(ref.dtype).itemsize == size
        pltpu.make_async_remote_copy(
            src_ref=ref, dst_ref=ref, send_sem=send_sem.at[n], recv_sem=recv_sem.at[0],
            device_id=peer, device_id_type=MESH).wait_send()


PIECES = 4
OUT = pltpu.VMEM
SENDS = 19
RECEIVES = 150


def body(queries, keys, values, cotangent):
    vmem = pl.BlockSpec(memory_space=pltpu.VMEM)
    hbm = pl.BlockSpec(memory_space=pl.ANY)
    return pl.pallas_call(
        kernel,
        name="memory_backward",
        out_shape=(
            OUT((2, D), BF),
            OUT((SL, D), BF),
            OUT((SL, D), BF),
        ),
        in_specs=[vmem, vmem, hbm, hbm],
        out_specs=(vmem, vmem, vmem),
        scratch_shapes=[
            pltpu.VMEM((NZ, 2, NX, NY, 16, F), BF),
            pltpu.VMEM((2, NDP, 2, 64, D), BF),
            pltpu.VMEM((2, 2, SL, D), BF),
            pltpu.VMEM((2 * SL, 128), F32),
            pltpu.VMEM((256, 256), BF),
            pltpu.VMEM((256, 256), BF),
            pltpu.VMEM((128, 2 * SL), BF),
            pltpu.VMEM((NDP, 2, SL, 128), BF),
            pltpu.VMEM((NDP, 2, SL, 128), BF),
            pltpu.VMEM((2 * SL, 128), F32),
            pltpu.VMEM((2 * SL, 128), F32),
            pltpu.VMEM((NY, 8, 128), F32),
            pltpu.VMEM((2 * NX, 8, 128), F32),
            pltpu.VMEM((NDP, 8, 128), F32),
            pltpu.VMEM((2, NX, 16, D), BF),
            pltpu.VMEM((2, 2, 16, D // 2), BF),
            pltpu.VMEM((2, 2, 16, D), BF),
            pltpu.VMEM((256, F), BF),
            pltpu.VMEM((NY - 1, 32, F), BF),
            pltpu.VMEM((3, 16, F), BF),
            pltpu.VMEM((2, SL, D), F32),
            pltpu.VMEM((2, SL, D), BF),
            pltpu.VMEM((2, SL, D), BF),
            pltpu.SemaphoreType.DMA((SENDS,)),
            pltpu.SemaphoreType.DMA((RECEIVES,)),
            pltpu.SemaphoreType.DMA((2,)),
        ],
        compiler_params=pltpu.CompilerParams(
            collective_id=0, has_side_effects=True, vmem_limit_bytes=56 * 2**20
        ),
    )(queries, cotangent, keys, values)


def solution(mesh):
    rows = P(("dp", "slot"), None)
    slots = P("slot", None)
    return jax.shard_map(
        body,
        mesh=mesh,
        in_specs=(rows, slots, slots, rows),
        out_specs=(rows, slots, slots),
        check_vma=False,
    )
```

```python
import math

import jax
import jax.numpy as jnp
from jax import lax
from jax.experimental import pallas as pl
from jax.experimental.pallas import tpu as pltpu
from jax.sharding import PartitionSpec as P

MESH = pl.DeviceIdType.MESH
D = 4096
BETA = 1.25 * D ** (-0.5)
NX, NY, NZ, NDP = 4, 8, 8, 4
SL = 160
F = 512
NF = D // F
BF = jnp.bfloat16
F32 = jnp.float32


UNITS = (
    (0, 0, "xy"),
    (0, 1, "yx"),
    (4, 0, "xy"),
    (4, 1, "yx"),
    (3, 0, "xy"),
    (3, 1, "yx"),
    (-3, 0, "xy"),
    (-3, 1, "yx"),
    (2, 0, "xy"),
    (-2, 1, "yx"),
)
RANKS = {
    "first": {(-3, 0): 6, (-3, 1): 0, (-2, 1): 0.5, (0, 0): 0, (0, 1): 6, (2, 0): 6, (3, 0): 1, (3, 1): 2, (4, 0): 7, (4, 1): 3},
    "line": {(-3, 0): 7, (-3, 1): 5, (-2, 1): 0, (0, 0): 3, (0, 1): 8, (2, 0): 8, (3, 0): 4, (3, 1): 2, (4, 0): 0, (4, 1): 0.5},
    "z1": {(-3, 0): 3, (-3, 1): 5, (-2, 0): 4, (2, 1): 4, (3, 0): 2, (3, 1): 4, (4, 0): 1, (4, 1): 2},
    "zf": {(-1, 0): 5, (1, 0): 7},
    "zl": {(-1, 0): 5, (-1, 1): 2, (1, 0): 4, (1, 1): 0.5},
}


def rank_of(kind, offset, array):
    return RANKS.get(kind, {}).get((offset, array), 1)


HOP_US = 2.3
FAR_US = 0.4
CORE_HOP_US = 1.5
LINK_RATE = 48e3
CORE_RATE = 500e3
BACKLOG_US = 0.7
START_US = 0.05
WAIT_US = 0.03


class Plan:
    def __init__(self):
        self.items = {}

        self.members = {}

    def transfer(self, name, needs, link, size, hops=1, rank=0, group=None):
        group = group or name
        self.members.setdefault(group, []).append(name)
        self.items[name] = dict(kind="t", needs=list(needs), link=link, size=size, hops=hops, rank=rank, group=group)

    def compute(self, name, needs, cost, rank=0):
        self.items[name] = dict(kind="c", needs=list(needs), cost=cost, rank=rank)

    def order(self):
        now = 0.0
        done, started, landing, arrivals, free, steps = set(), set(), {}, {}, {}, []
        group_of = {n: i.get("group", n) for n, i in self.items.items()}
        needs = {n: {group_of[d] for d in i["needs"]} for n, i in self.items.items()}
        left = set(group_of.values())
        while left:
            ready = [n for n in self.items if n not in started and needs[n] <= done]
            held = []
            sends = sorted((n for n in ready if self.items[n]["kind"] == "t"), key=lambda n: self.items[n]["rank"])
            for n in sends:
                i = self.items[n]
                rate, hop = (CORE_RATE, CORE_HOP_US) if i["link"] == "core" else (LINK_RATE, HOP_US)
                links = [i["link"][0] + w for w in "+-"] if i["link"].endswith("*") else [i["link"]]
                queued = max(free.get(link, 0.0) for link in links)
                if queued - now > BACKLOG_US and i["rank"] > 0:
                    held.append(queued - BACKLOG_US)
                    continue
                now += START_US
                for link in links:
                    free[link] = max(now, free.get(link, 0.0)) + i["size"] * i["hops"] / rate / len(links)
                landing[n] = max(free[link] for link in links) + hop + FAR_US * (i["hops"] - 1)
                started.add(n)
                steps.append(("start", n))
                group = i["group"]
                if all(m in started for m in self.members[group]):
                    arrivals[group] = max(landing[m] for m in self.members[group])
            first = min(arrivals, key=lambda n: (arrivals[n], str(n))) if arrivals else None
            if first is not None and arrivals[first] <= now:
                steps.append(("wait", first))
                arrivals.pop(first)
                done.add(first)
                left.discard(first)
                now += WAIT_US
                continue
            runs = sorted((n for n in ready if self.items[n]["kind"] == "c"), key=lambda n: self.items[n]["rank"])
            if runs:
                n = runs[0]
                now += self.items[n]["cost"]
                started.add(n)
                done.add(n)
                left.discard(n)
                steps.append(("run", n))
                continue
            if held and (first is None or min(held) < arrivals[first]):
                now = max(now, min(held)) + 0.001
                continue
            now = max(now, arrivals.pop(first)) + WAIT_US
            steps.append(("wait", first))
            done.add(first)
            left.discard(first)
        self.end = now
        return steps


def kernel(q_ref, g_ref, k_hbm, v_hbm, qg_ref, kg_ref, vg_ref,
           blocks, rows, kv, norm, spread, gather_rows, turned, probs, dscores, scores, dprobs,
           stat_y, stat_x, stat_f, rs, rs_a, rs_x, rs_t, rs_y, rs_z, own, cross, landed,
           send_sem, recv_sem, load_sem):
    dp = lax.axis_index("dp")
    slot = lax.axis_index("slot")
    c = slot % 2
    y = (slot // 2) % NY
    zh = (slot // 16) % 2
    x = slot // 32
    z = zh * NDP + dp

    def chip(dx, dy, dz):
        zz = (z + dz + NZ) % NZ
        return {"dp": zz % NDP, "slot": ((((x + dx + NX) % NX) * 2 + zz // NDP) * NY + (y + dy + NY) % NY) * 2 + c}

    other_core = {"dp": dp, "slot": slot + 1 - 2 * c}

    loads = []
    for n, src in enumerate((k_hbm, v_hbm)):
        cp = pltpu.make_async_copy(src, kv.at[n, c], load_sem.at[n])
        cp.start()
        loads.append(cp)

    barrier = pltpu.get_barrier_semaphore()
    peers = [chip(d, 0, 0) for d in range(1, NX)] + [chip(0, d, 0) for d in range(1, NY)]
    peers += [chip(0, 0, d) for d in range(1, NZ)] + [chip(d, 0, 4) for d in range(1, NX)] + [other_core]
    for p in peers:
        pl.semaphore_signal(barrier, inc=1, device_id=p, device_id_type=MESH)

    def to_rows16(ref):
        wide = ref[...].astype(F32)
        return jnp.concatenate([wide[r:r + 1, i * F:(i + 1) * F] for r in range(2) for i in range(NF)], axis=0).astype(BF)

    blocks[z, 0, x, y] = to_rows16(q_ref)
    blocks[z, 1, x, y] = to_rows16(g_ref)

    row = lax.broadcasted_iota(jnp.int32, (256, 256), 0)
    col = lax.broadcasted_iota(jnp.int32, (256, 256), 1)
    spread[...] = jnp.where(col == (row % 32) * NF + row // 32, 1.0, 0.0).astype(BF)
    want = (row % 8) * 32 + ((row // 16) % 2) * 16 + (row // 32) * 2 + (row // 8) % 2
    gather_rows[...] = jnp.where(col == want, 1.0, 0.0).astype(BF)

    pl.semaphore_wait(barrier, len(peers))

    plan = Plan()
    emit = {}
    send_index = {}
    recv_index = {}
    sent = {}

    def transfer(name, needs, link, size, src, dst, incoming, peer, hops=1, rank=0, group=None, whole=None, drain=None):
        plan.transfer(name, needs, link, size, hops, rank, group)
        r = recv_index.setdefault(group or name, len(recv_index))
        key, view = drain or (name, src)
        n = send_index.setdefault(key, len(send_index))
        if size:
            sent.setdefault(key, [view, n, peer, 0])[3] += size

        def out():
            return pltpu.make_async_remote_copy(
                src_ref=src(), dst_ref=dst(), send_sem=send_sem.at[n], recv_sem=recv_sem.at[r],
                device_id=peer, device_id_type=MESH)

        def into():
            ref = (whole or incoming)()
            return pltpu.make_async_remote_copy(
                src_ref=ref, dst_ref=ref, send_sem=send_sem.at[n], recv_sem=recv_sem.at[r],
                device_id=peer, device_id_type=MESH)

        emit[name] = (out, into)
        if group:
            emit[group] = (out, into)

    def compute(name, needs, cost, run, rank=0):
        plan.compute(name, needs, cost, rank)
        emit[name] = run

    def at(dz, a, dx, dy):
        xs = dx if not isinstance(dx, int) else (x + dx + NX) % NX
        ys = dy if not isinstance(dy, int) else (y + dy + NY) % NY
        return blocks.at[(z + dz + NZ) % NZ, a, xs, ys]

    def unit(dz, a):
        return blocks.at[(z + dz + NZ) % NZ, a]

    def move(name, needs, link, size, dz, a, dx, dy, step, hops=1, rank=0, **names):
        ex, ey, ez = step

        def shifted(d, e):
            return d if not isinstance(d, int) else d - e

        transfer(name, needs, link, size, lambda: at(dz, a, dx, dy), lambda: at(dz, a, dx, dy),
                 lambda: at(dz - ez, a, shifted(dx, ex), shifted(dy, ey)), chip(*step), hops, rank, **names)

    KIB = 1024
    every = slice(None)

    def of_unit(dz, a, part=None):
        if dz == 0 and a == 0:
            if part == "xp":
                return "own xp", lambda: blocks.at[0, 0, 0, pl.ds(0, 3)]
            return "own yl", lambda: blocks.at[0, 0, :, pl.ds(0, 7)]
        return ("unit", dz, a,), lambda: unit(dz, a)

    for ez, a in ((4, 0), (4, 1), (-3, 0), (3, 0), (-3, 1), (3, 1), (-2, 0), (2, 1)):
        move(("z1", ez, a,), [], "z*" if ez == 4 else "z+" if ez > 0 else "z-", 16 * KIB, 0, a, 0, 0, (0, 0, ez),
             hops=abs(ez), rank=rank_of("z1", ez, a), drain=of_unit(4 if ez == 4 else -ez, a))

    def first_hop(dz, a):
        return [] if dz == 0 else [("z1", 4, a,) if dz == 4 else ("z1", -dz, a,)]

    def line_parts(dz):
        return (0, 1) if dz in (0, 4) else (None,)

    arrived = {(dz, a): [] for dz in range(-3, 5) for a in range(2)}
    for u, (dz, a, route) in enumerate(UNITS):
        have = first_hop(dz, a)
        near = dz in (0, 4)
        first, rank = rank_of("first", dz, a), rank_of("line", dz, a)
        firsts = []
        if route == "xy":
            for e in (1, -1, 2):
                name = ("xp", dz, a, e,)
                move(name, have, "x*" if e == 2 else "x-" if e < 0 else "x+", 16 * KIB, dz, a, 0, 0, (e, 0, 0), hops=abs(e), rank=first,
                     group=("xp", dz, a,), whole=lambda: blocks.at[0, 0, 0, pl.ds(0, 3)], drain=of_unit(dz, a, "xp"))
                firsts.append(name)
            for k in range(4):
                for way in (1, -1):
                    for h in line_parts(dz):
                        if k == 3 and h == (1 if way > 0 else 0):
                            continue
                        needs = firsts + have if k == 0 else [("yl", dz, a, way, k - 1, h,)]
                        half = (pl.ds(0, 2) if way > 0 else pl.ds(2, 2)) if k == 3 else every if h is None else pl.ds(2 * h, 2)
                        name = ("yl", dz, a, way, k, h,)
                        move(name, needs, "y+" if way > 0 else "y-", (64 if k < 3 and h is None else 32) * KIB,
                             dz, a, half, -way * k, (0, way, 0), rank=rank, drain=of_unit(dz, a))
                        arrived[dz, a].append(name)
        else:
            if near:
                for d in range(1, NY):
                    name = ("yp", dz, a, d,)
                    move(name, have, "y*" if d == 4 else "y+" if d < 4 else "y-", 16 * KIB, dz, a, 0, 0, (0, d, 0), hops=min(d, NY - d), rank=first,
                         group=("yp", dz, a,), whole=lambda: blocks.at[0, 0, 0, pl.ds(0, 7)], drain=of_unit(dz, a))
                    firsts.append(name)
            else:
                for way in (1, -1):
                    for k in range(4 if (way > 0) == (u % 4 == 1) else 3):
                        name = ("yp", dz, a, way, k,)
                        needs = have if k == 0 else [("yp", dz, a, way, k - 1,)]
                        move(name, needs, "y+" if way > 0 else "y-", 16 * KIB, dz, a, 0, -way * k, (0, way, 0), rank=first,
                             drain=of_unit(dz, a))
                        firsts.append(name)
            for e in (1, -1):
                for k in range(2):
                    needs = firsts + have if k == 0 else [("xl", dz, a, e, 0,)]
                    name = ("xl", dz, a, e, k,)
                    half = every if k == 0 else (pl.ds(0, 4) if e > 0 else pl.ds(4, 4))
                    move(name, needs, "x+" if e > 0 else "x-", (128 if k == 0 else 64) * KIB, dz, a, -e * k, half,
                         (e, 0, 0), rank=rank, drain=of_unit(dz, a))
                    arrived[dz, a].append(name)
        arrived[dz, a] += firsts + have
        if dz == 0:
            own_line = (firsts if a == 0 else own_line[0], firsts)

    for ez in (1, -1):
        link = "z+" if ez > 0 else "z-"
        lines = [(0, ("own",), own_line[0], 64, every, 0), (1, ("own",), own_line[1], 128, 0, every)]
        for way in (1, -1):
            for k in range(4):
                half = every if k < 3 else (pl.ds(0, 2) if way > 0 else pl.ds(2, 2))
                needs = [n for n in arrived[0, 0] if n[:5] == ("yl", 0, 0, way, k)]
                lines.append((0, (way, k), needs, 64 if k < 3 else 32, half, -way * (k + 1)))
            for k in range(2):
                half = every if k < 1 else (pl.ds(0, 4) if way > 0 else pl.ds(4, 4))
                lines.append((1, (way, k), [("xl", 0, 1, way, k,)], 128 if k < 1 else 64, -way * (k + 1), half))
        for a, label, needs, size, dx, dy in lines:
            name = ("zl", a, ez, *label)
            passes = a == (0 if ez > 0 else 1)
            as_one = {} if passes else dict(group=("zl", a, ez,), whole=lambda ez=ez, a=a: unit(-ez, a))
            move(name, needs, link, size * KIB, 0, a, dx, dy, (0, 0, ez), rank=rank_of("zl", ez, a),
                 drain=(("zl", ez,), lambda: blocks.at[0]), **as_one)
            arrived[-ez, a].append(name)
            if passes:
                further = ("zf", a, ez, *label)
                move(further, [name], link, size * KIB, -ez, a, dx, dy, (0, 0, ez), rank=rank_of("zf", ez, 0), group=("zf", ez,),
                     whole=lambda ez=ez, a=a: unit(-2 * ez, a), drain=("zf", lambda: blocks.at[0]))
                arrived[-2 * ez, a].append(further)

    def load(n):
        return lambda: loads[n].wait()

    for n in range(2):
        compute(("load", n,), [], 0.6, load(n), rank=5)
        transfer(("kv", n,), [("load", n,)], "core", 1280 * KIB, lambda n=n: kv.at[n, c], lambda n=n: kv.at[n, c],
                 lambda n=n: kv.at[n, 1 - c], other_core, rank=9, drain=("kv", lambda: kv.at[:, c]))

    def key_norm():
        for half in range(2):
            def add(i, total):
                part = kv[0, half, :, pl.ds(pl.multiple_of(i * 128, 128), 128)].astype(F32)
                return total + part * part
            total = lax.fori_loop(0, D // 128, add, jnp.zeros((SL, 128), F32))
            norm[pl.ds(half * SL, SL), :] = jnp.broadcast_to(
                (0.5 * BETA) * jnp.sum(total, axis=1, keepdims=True), (SL, 128))

    compute("norm", [("load", 0), ("kv", 0)], 1.1, key_norm, rank=6)

    def relayout(dz, a):
        def run():
            zz = (z + dz + NZ) % NZ
            for h in range(2):
                got = blocks[zz, a, 2 * h:2 * h + 2].reshape(256, F)
                laid = jnp.dot(spread[...], got, preferred_element_type=F32).astype(BF)
                for i in range(NF):
                    rows[a, zz % NDP, zz // NDP, pl.ds(32 * h, 32), i * F:(i + 1) * F] = laid[i * 32:(i + 1) * 32]
        return run

    for dz in range(-3, 5):
        for a in range(2):
            compute(("rows", dz, a,), arrived[dz, a], 0.12, relayout(dz, a), rank=3 if dz in (0, 4) else 8)

    def products(group):
        def one(n):
            return lax.dot_general(kv[n].reshape(2 * SL, D), rows[n, group].reshape(128, D), (((1,), (1,)), ((), ())),
                                   preferred_element_type=F32)
        return BETA * one(0) - norm[...], one(1)

    def own_scores():
        s, d = products(dp)
        scores[...] = s
        dprobs[...] = d
        top = jnp.max(s, axis=0, keepdims=True)
        e = jnp.exp(s - top)
        stat_y[y, 0:1] = top
        stat_y[y, 1:2] = jnp.sum(e, axis=0, keepdims=True)
        stat_y[y, 2:3] = jnp.sum(e * d, axis=0, keepdims=True)
        stat_y[y, 3:8] = jnp.zeros((5, 128), F32)

    def merge(ref):
        parts = [ref[i] for i in range(8)]
        top = parts[0][0:1]
        for p in parts[1:]:
            top = jnp.maximum(top, p[0:1])
        total = jnp.zeros((1, 128), F32)
        weighted = jnp.zeros((1, 128), F32)
        for p in parts:
            scale = jnp.exp(p[0:1] - top)
            total += p[1:2] * scale
            weighted += p[2:3] * scale
        return top, total, weighted

    compute("own scores", [("rows", 0, 0), ("rows", 0, 1), ("rows", 4, 0), ("rows", 4, 1), "norm", ("load", 1), ("kv", 1)], 1.3, own_scores, rank=1)
    stats = ("stats", lambda: norm.at[pl.ds(0, 17 * 8)])
    for d in range(1, NY):
        transfer(("sy", d,), ["own scores"], "s", 4 * KIB, lambda: stat_y.at[y], lambda: stat_y.at[y],
                 lambda: stat_y.at[0], chip(0, d, 0), rank=-5,
                 group="sy", whole=lambda: stat_y.at[pl.ds(0, 7)], drain=stats)

    place = x * 2 + zh

    def merge_y():
        top, total, weighted = merge(stat_y)
        stat_x[place, 0:1] = top
        stat_x[place, 1:2] = total
        stat_x[place, 2:3] = weighted
        stat_x[place, 3:8] = jnp.zeros((5, 128), F32)

    compute("merge y", [("sy", d,) for d in range(1, NY)], 0.3, merge_y, rank=0)
    for d in range(NX):
        for e in range(2):
            if d or e:
                transfer(("sx", d, e,), ["merge y"], "s", 4 * KIB, lambda: stat_x.at[place], lambda: stat_x.at[place],
                         lambda: stat_x.at[0], chip(d, 0, 4 * e), rank=-5,
                         group="sx", whole=lambda: stat_x.at[pl.ds(0, 7)], drain=stats)

    def merge_x():
        top, total, weighted = merge(stat_x)
        stat_f[dp, 0:1] = top + jnp.log(total)
        stat_f[dp, 1:2] = weighted / total
        stat_f[dp, 2:8] = jnp.zeros((6, 128), F32)

    compute("merge x", [("sx", d, e,) for d in range(NX) for e in range(2) if d or e], 0.3, merge_x, rank=0)
    for d in range(1, NDP):
        transfer(("sf", d,), ["merge x"], "s", 4 * KIB, lambda: stat_f.at[dp], lambda: stat_f.at[dp],
                 lambda: stat_f.at[0], {"dp": (dp + d) % NDP, "slot": slot}, rank=-5,
                 group="sf", whole=lambda: stat_f.at[pl.ds(0, 3)], drain=stats)

    def weights(group, s, d):
        lse = stat_f[group, 0:1]
        delta = stat_f[group, 1:2]
        prob = jnp.exp(s - lse)
        dscore = (BETA * prob * (d - delta)).astype(BF)
        probs[group] = prob.astype(BF).reshape(2, SL, 128)
        dscores[group] = dscore.reshape(2, SL, 128)
        return dscore

    def own_weights():
        dscore = weights(dp, scores[...], dprobs[...])
        turned[...] = dscore.astype(F32).T.astype(BF)

    def query_part(h):
        def part(i, _):
            cut = pl.ds(pl.multiple_of(i * F, F), F)
            out = jnp.dot(turned[...], kv[0, :, :, cut].reshape(2 * SL, F), preferred_element_type=F32)
            rs[:, :, :, cut] = out.astype(BF).reshape(2, NX, 16, F)
            return 0
        lax.fori_loop(h * NF // 2, (h + 1) * NF // 2, part, 0)

    compute("own weights", ["merge x"], 0.4, own_weights, rank=0)
    for h in range(2):
        compute(("query", "part", h,), ["own weights"], 0.6, lambda h=h: query_part(h), rank=0)
    parts = ("parts", lambda: rs.at[:, pl.ds(0, 3)])
    low, high = slice(0, D // 2), slice(D // 2, D)
    for e, far, near in ((1, low, high), (-1, high, low)):
        link = "x+" if e > 0 else "x-"
        slot_in = 0 if e > 0 else 1
        transfer(("ra", e,), [("query", "part", 0 if e > 0 else 1,)], link, 128 * KIB, lambda far=far: rs.at[:, (x + 2) % NX, :, far],
                 lambda s=slot_in: rs_a.at[s], lambda s=slot_in: rs_a.at[s], chip(e, 0, 0), rank=-2, drain=parts)
        transfer(("rb", e, 0,), [("query", "part", 1 if e > 0 else 0,)], link, 128 * KIB, lambda e=e, near=near: rs.at[:, (x + e + NX) % NX, :, near],
                 lambda s=slot_in, near=near: rs_x.at[s, :, :, near], lambda s=slot_in, near=near: rs_x.at[s, :, :, near],
                 chip(e, 0, 0), rank=-1, drain=parts)

        def add(e=e, far=far, slot_in=slot_in):
            to = (x + e + NX) % NX
            for i in range(NF // 2):
                cut = slice(far.start + i * F, far.start + (i + 1) * F)
                both = rs[:, to, :, cut].astype(F32) + rs_a[slot_in, :, :, i * F:(i + 1) * F].astype(F32)
                rs[:, to, :, cut] = both.astype(BF)

        compute(("add", e,), [("ra", e,)], 0.2, add, rank=0)
        transfer(("rb", e, 1,), [("add", e,)], link, 128 * KIB, lambda e=e, far=far: rs.at[:, (x + e + NX) % NX, :, far],
                 lambda s=slot_in, far=far: rs_x.at[s, :, :, far], lambda s=slot_in, far=far: rs_x.at[s, :, :, far],
                 chip(e, 0, 0), rank=-1, drain=parts)

    def reduce_x():
        for i in range(NF):
            cut = slice(i * F, (i + 1) * F)
            total = rs[:, x, :, cut].astype(F32) + rs_x[0, :, :, cut].astype(F32) + rs_x[1, :, :, cut].astype(F32)
            rs_t[pl.ds(32 * i, 32), :] = total.reshape(32, F).astype(BF)
        laid = jnp.dot(gather_rows[...], rs_t[...], preferred_element_type=F32).astype(BF)
        rs_t[...] = laid

    compute("reduce x", [("rb", e, k,) for e in (1, -1) for k in range(2)], 0.6, reduce_x, rank=0)
    for d in (4, 3, 5, 2, 6, 1, 7):
        transfer(("ry", d,), ["reduce x"], "y*" if d == 4 else "y+" if d < 4 else "y-", 32 * KIB,
                 lambda d=d: rs_t.at[pl.ds(pl.multiple_of(((y + d) % NY) * 32, 32), 32)],
                 lambda d=d: rs_y.at[d - 1], lambda d=d: rs_y.at[d - 1], chip(0, d, 0), hops=min(d, NY - d), rank=-3,
                 group="ry", whole=lambda: rs_y, drain=("ry", lambda: rs_y))

    def reduce_y():
        total = rs_t[pl.ds(pl.multiple_of(y * 32, 32), 32), :].astype(F32)
        for d in range(NY - 1):
            total += rs_y[d].astype(F32)
        rs_z[0:2] = total.astype(BF).reshape(2, 16, F)

    compute("reduce y", [("ry", d,) for d in range(1, NY)], 0.3, reduce_y, rank=0)
    transfer("rz", ["reduce y"], "z*", 16 * KIB, lambda: rs_z.at[1 - zh], lambda: rs_z.at[2], lambda: rs_z.at[2],
             chip(0, 0, 4), hops=4, rank=-3, drain=of_unit(0, 1))

    def finish_queries():
        total = rs_z[zh].astype(F32) + rs_z[2].astype(F32)
        lines = [jnp.concatenate([total[8 * r + i:8 * r + i + 1] for i in range(NF)], axis=1) for r in range(2)]
        qg_ref[...] = jnp.concatenate(lines, axis=0).astype(BF)

    compute("finish queries", ["rz"], 0.2, finish_queries, rank=12)

    def other_group(k):
        def run():
            group = (dp + k) % NDP
            s, d = products(group)
            weights(group, s, d)
        return run

    for k in range(1, NDP):
        zs = [k, k - 4]
        compute(("group", k,), [("rows", d, a,) for d in zs for a in range(2)] + [("sf", NDP - k,), "norm", ("load", 1), ("kv", 1)],
                1.3, other_group(k), rank=7)

    def gradients(core, j, store):
        left_k = jnp.concatenate([dscores[i, core] for i in range(NDP)], axis=1)
        left_v = jnp.concatenate([probs[i, core] for i in range(NDP)], axis=1)
        column = jnp.sum(left_k.astype(F32), axis=1, keepdims=True)
        for i in range(j * NF // PIECES, (j + 1) * NF // PIECES):
            cut = slice(i * F, (i + 1) * F)
            grad = jnp.dot(left_k, rows[0, :, :, :, cut].reshape(512, F), preferred_element_type=F32)
            store(i, 0, grad - column * kv[0, core, :, cut].astype(F32))
            store(i, 1, jnp.dot(left_v, rows[1, :, :, :, cut].reshape(512, F), preferred_element_type=F32))

    groups = [("group", k) for k in range(1, NDP)] + ["own weights"]
    wide = D // PIECES

    def store_in(ref):
        def store(i, n, value):
            ref[n, :, i * F:(i + 1) * F] = value.astype(ref.dtype)
        return store

    def finish(j):
        for i in range(j * NF // PIECES, (j + 1) * NF // PIECES):
            cut = slice(i * F, (i + 1) * F)
            for n, ref in enumerate((kg_ref, vg_ref)):
                ref[:, cut] = (own[n, :, cut] + landed[n, :, cut].astype(F32)).astype(BF)

    for j in range(PIECES):
        cut = pl.ds(j * wide, wide)
        compute(("other", j), groups, 0.3, lambda j=j: gradients(1 - c, j, store_in(cross)), rank=20)
        transfer(("cx", j), [("other", j)], "core", 2 * SL * wide * 2, lambda cut=cut: cross.at[:, :, cut],
                 lambda cut=cut: landed.at[:, :, cut], lambda cut=cut: landed.at[:, :, cut], other_core, rank=0,
                 drain=("cx", lambda: cross))
        compute(("own", j), groups, 0.3, lambda j=j: gradients(c, j, store_in(own)), rank=21)
        compute(("finish", j), [("own", j), ("cx", j)], 0.2, lambda j=j: finish(j), rank=22)

    assert len(recv_index) <= RECEIVES and len(send_index) <= SENDS
    for what, name in plan.order():
        if what == "start":
            emit[name][0]().start()
        elif what == "wait":
            emit[name][1]().wait_recv()
        else:
            emit[name]()

    for view, n, peer, size in sent.values():
        ref = view()
        assert math.prod(ref.shape) * jnp.dtype(ref.dtype).itemsize == size
        pltpu.make_async_remote_copy(
            src_ref=ref, dst_ref=ref, send_sem=send_sem.at[n], recv_sem=recv_sem.at[0],
            device_id=peer, device_id_type=MESH).wait_send()


PIECES = 4
OUT = pltpu.VMEM
SENDS = 19
RECEIVES = 150


def body(queries, keys, values, cotangent):
    vmem = pl.BlockSpec(memory_space=pltpu.VMEM)
    hbm = pl.BlockSpec(memory_space=pl.ANY)
    return pl.pallas_call(
        kernel,
        name="memory_backward",
        out_shape=(
            OUT((2, D), BF),
            OUT((SL, D), BF),
            OUT((SL, D), BF),
        ),
        in_specs=[vmem, vmem, hbm, hbm],
        out_specs=(vmem, vmem, vmem),
        scratch_shapes=[
            pltpu.VMEM((NZ, 2, NX, NY, 16, F), BF),
            pltpu.VMEM((2, NDP, 2, 64, D), BF),
            pltpu.VMEM((2, 2, SL, D), BF),
            pltpu.VMEM((2 * SL, 128), F32),
            pltpu.VMEM((256, 256), BF),
            pltpu.VMEM((256, 256), BF),
            pltpu.VMEM((128, 2 * SL), BF),
            pltpu.VMEM((NDP, 2, SL, 128), BF),
            pltpu.VMEM((NDP, 2, SL, 128), BF),
            pltpu.VMEM((2 * SL, 128), F32),
            pltpu.VMEM((2 * SL, 128), F32),
            pltpu.VMEM((NY, 8, 128), F32),
            pltpu.VMEM((2 * NX, 8, 128), F32),
            pltpu.VMEM((NDP, 8, 128), F32),
            pltpu.VMEM((2, NX, 16, D), BF),
            pltpu.VMEM((2, 2, 16, D // 2), BF),
            pltpu.VMEM((2, 2, 16, D), BF),
            pltpu.VMEM((256, F), BF),
            pltpu.VMEM((NY - 1, 32, F), BF),
            pltpu.VMEM((3, 16, F), BF),
            pltpu.VMEM((2, SL, D), F32),
            pltpu.VMEM((2, SL, D), BF),
            pltpu.VMEM((2, SL, D), BF),
            pltpu.SemaphoreType.DMA((SENDS,)),
            pltpu.SemaphoreType.DMA((RECEIVES,)),
            pltpu.SemaphoreType.DMA((2,)),
        ],
        compiler_params=pltpu.CompilerParams(
            collective_id=0, has_side_effects=True, vmem_limit_bytes=56 * 2**20
        ),
    )(queries, cotangent, keys, values)


def solution(mesh):
    rows = P(("dp", "slot"), None)
    slots = P("slot", None)
    return jax.shard_map(
        body,
        mesh=mesh,
        in_specs=(rows, slots, slots, rows),
        out_specs=(rows, slots, slots),
        check_vma=False,
    )
```
